128 devices in a mesh: seq: 2 (over core), fsdp: 64 (over z, y, x).
Axes of the slice: x: 4, y: 4, z: 4, core: 2. Of those that a mesh axis runs over, the one named last changes fastest.
Arguments:
- tokens: bfloat16 [64, 256, 4096], P('fsdp', 'seq'), may hold values from -6 to 6
- weight: bfloat16 [4096, 10240], P('fsdp', 'seq'), may hold values from -4 to 4
- adapter_down_weight: bfloat16 [4096, 4, 16], P('fsdp'), may hold values from -0.09375 to 0.09375
- adapter_up_weight: bfloat16 [4, 16, 10240], P(None, None, 'seq'), may hold values from -1.5 to 1.5
- magnitude: float32 [4, 10240], P(None, 'seq'), may hold values from 0.25 to 1.75
- step_size_weight: bfloat16 [4096, 128], P('fsdp'), may hold values from -0.09375 to 0.09375
- step_size_bias: float32 [128], replicated, may hold values from -1 to 1
- decay_rate_log: float32 [128], replicated, may hold values from -12 to -2
- head_skip_gain: float32 [128], replicated, may hold values from 0.5 to 1.5
- convolution_weight: float32 [4, 10240], replicated, may hold values from -3 to 3
- convolution_bias: float32 [10240], replicated, may hold values from -3 to 3
- grouped_norm_gain: float32 [8192], replicated, may hold values from 0.25 to 1.75
- tenant: int32 [64], P('fsdp'), may hold values from 0 to 3
- lengths: int32 [64], P('fsdp'), may hold values from 1 to 256, 10240 in all
- cotangent: bfloat16 [64, 256, 8192], P('fsdp', 'seq'), may hold values from -6 to 6
Outputs:
- mixed: bfloat16 [64, 256, 8192], P('fsdp', 'seq')
- x_grad: bfloat16 [64, 256, 8192], P('fsdp', 'seq')
The draws below stay inside these ranges and needn't reach their ends.
All inputs are finite; a program needn't handle non-finite values. No bound on the sum of `lengths` on one device may be relied on, other than what follows from the above.
Results may differ from the reference program's by a relative error of at most 0.0075.
Values may be sent and summed in bfloat16 or wider, within the bound.
No kernel may reach another device: no remote copies, remote signals or barrier semaphores. Data moves between devices by JAX's collectives and lax.ppermute only.
A program may use at most 192 MiB of HBM per device.

```python
import math
import jax
import jax.numpy as jnp
import numpy as np
from jax import lax

MODEL_WIDTH = 4096
HEADS = 128
HEAD_DIM = 64
GROUPS = 8
STATE = 128
TENANT_COUNT = 4
ADAPTER_RANK = 16
CONV = 4
SPAN = 128
XCH = 8192
CONV_COLUMNS = 10240
LEN = 256
SEQS = 64


def draw_weight(key, part):
    key = jax.random.fold_in(key, 5)
    key_base, key_rows, key_cols = jax.random.split(key, 3)
    position = jnp.arange(MODEL_WIDTH, dtype=jnp.float32) / MODEL_WIDTH
    col_scale = jnp.exp(jax.random.uniform(key_cols, (CONV_COLUMNS,), jnp.float32, math.log(0.5), math.log(2.0)))
    spread = jnp.exp(jax.random.uniform(key_rows, (MODEL_WIDTH,), jnp.float32, 0.0, math.log(10.0)))
    row_scale = jnp.exp(position * 0.5 * math.log(3.0)) * spread
    entries = jnp.clip(jax.random.normal(key_base, (MODEL_WIDTH, CONV_COLUMNS), jnp.float32), -4.0, 4.0)
    values = entries * row_scale[:, None] * col_scale[None, :] / (6.0 * math.sqrt(MODEL_WIDTH))
    return jnp.clip(values, -4.0, 4.0).astype(jnp.bfloat16)


def draw_decay_rate_log(key, part):
    key = jax.random.fold_in(key, 11)
    key_pick, key_slow, key_fast = jax.random.split(key, 3)
    fast_share = 0.5
    fast = jax.random.uniform(key_pick, (HEADS,), jnp.float32) < fast_share
    slow_rate = jax.random.uniform(key_slow, (HEADS,), jnp.float32, math.log(0.2 / LEN), math.log(1.2 / LEN))
    fast_rate = jax.random.uniform(key_fast, (HEADS,), jnp.float32, math.log(1.0 / 50.0), math.log(1.0 / 20.0))
    return jnp.where(fast, fast_rate, slow_rate)


def with_ends(values, key, low, largest):
    shape = values.shape
    place = [jax.random.randint(jax.random.fold_in(key, axis), (), 0, shape[axis]) for axis in range(len(shape))]
    values = values.at[tuple(place)].set(low)
    longest = shape.index(max(shape))
    place[longest] = (place[longest] + 1) % shape[longest]
    return values.at[tuple(place)].set(largest)


def steps_of(own_key, dims, shards, low, high):
    factor_of, own = 1.0, jax.random.fold_in(own_key, 6)
    for dim, parts in shards:
        heights = jnp.exp(jax.random.uniform(jax.random.fold_in(own, dim), (parts,), jnp.float32, low / len(shards), high / len(shards)))
        factor_of = factor_of * jnp.repeat(heights, dims[dim] // parts).reshape([-1 if axis == dim else 1 for axis in range(len(dims))])
    return factor_of


def split_up(amount, total, limit, skew):
    portions = [(1 << 20) // math.isqrt(standing ** skew) + 1 for standing in range(2, amount + 1)]
    spare, given = total - limit - (amount - 1), [1] * (amount - 1)
    while spare > 0:
        candidates = [i for i in range(amount - 1) if given[i] < limit]
        mass, budget = sum([portions[i] for i in candidates]), spare
        for i in candidates:
            more = min(limit - given[i], max(1, budget * portions[i] // mass), spare)
            given[i] = given[i] + more
            spare = spare - more
    return np.array([limit] + given)


def uneven(rng, amount, total, most, slope):
    if amount == 2:
        one = jax.random.randint(rng, (), max(1, total - most), min(most, total - 1) + 1)
        return jnp.stack([one, total - one])
    sizes = jnp.asarray(split_up(amount, total, most, slope), jnp.int32)
    pairs = (amount - 1) // 2
    donor, sink = sizes[1:1 + 2 * pairs:2], sizes[2:2 + 2 * pairs:2]
    margin = jnp.minimum(donor - 1, most - sink)
    passed = jax.random.randint(jax.random.fold_in(rng, 1), (pairs,), 0, 1 << 20) % (margin + 1)
    sizes = sizes.at[1:1 + 2 * pairs:2].set(donor - passed).at[2:2 + 2 * pairs:2].set(sink + passed)
    return sizes[jax.random.permutation(jax.random.fold_in(rng, 2), amount)]


def noise(rng, dims, deviation, most, pieces=(), held_as=jnp.bfloat16):
    gain = steps_of(rng, dims, pieces, -0.22, 0.18) if pieces else 1.0
    result = jax.random.normal(rng, dims, jnp.float32) * deviation * gain
    return jnp.minimum(jnp.maximum(result, -most), most).astype(held_as)


def setup_inputs(seed: int = 0) -> dict:
    key_of = jax.random.split(jax.random.key(seed), 16)
    return {
        "tokens": noise(key_of[0], (SEQS, LEN, MODEL_WIDTH), 1.0, 6.0, ((0, 64), (1, 2))),
        "weight": draw_weight(jax.random.fold_in(key_of[15], 71), 0),
        "adapter_down_weight": noise(key_of[2], (MODEL_WIDTH, TENANT_COUNT, ADAPTER_RANK), MODEL_WIDTH ** -0.5, 0.09375, ((0, 64),)),
        "adapter_up_weight": noise(key_of[3], (TENANT_COUNT, ADAPTER_RANK, CONV_COLUMNS), ADAPTER_RANK ** -0.5, 1.5, ((2, 2),)),
        "magnitude": jnp.clip(1.0 + 0.15 * jax.random.normal(key_of[4], (TENANT_COUNT, CONV_COLUMNS), jnp.float32), 0.25, 1.75),
        "step_size_weight": noise(key_of[5], (MODEL_WIDTH, HEADS), MODEL_WIDTH ** -0.5, 0.09375, ((0, 64),)),
        "step_size_bias": jnp.clip(jax.random.uniform(key_of[6], (HEADS,), jnp.float32, -1.0, 1.0), -1.0, 1.0),
        "decay_rate_log": draw_decay_rate_log(jax.random.fold_in(key_of[15], 71), 0),
        "head_skip_gain": jnp.clip(jax.random.uniform(key_of[8], (HEADS,), jnp.float32, 0.5, 1.5), 0.5, 1.5),
        "convolution_weight": noise(key_of[9], (CONV, CONV_COLUMNS), CONV ** -0.5, 3.0, (), jnp.float32),
        "convolution_bias": noise(key_of[10], (CONV_COLUMNS,), 0.5, 3.0, (), jnp.float32),
        "grouped_norm_gain": jnp.clip(1.0 + 0.15 * jax.random.normal(key_of[11], (XCH,), jnp.float32), 0.25, 1.75),
        "tenant": with_ends(jax.random.randint(key_of[12], (SEQS,), 0, TENANT_COUNT), jax.random.fold_in(key_of[12], 1), 0, TENANT_COUNT - 1).astype(jnp.int32),
        "lengths": uneven(key_of[13], SEQS, SEQS * LEN * 5 // 8, LEN, 1).astype(jnp.int32),
        "cotangent": noise(key_of[14], (SEQS, LEN, XCH), 1.0, 6.0, ((0, 64), (1, 2))),
    }


eps_norm = 1e-05
eps_column = 1e-06

def span_terms(logdecay, inflow, b_keys, c_queries):
    blocks, block_len, head_count = logdecay.shape
    groups = b_keys.shape[2]
    per_group = head_count // groups
    channels = inflow.shape[3]
    cumul_log = jnp.cumsum(logdecay, axis=1)
    block_total = cumul_log[:, -1, :]
    scores = jnp.einsum('ctgn,csgn->cgts', c_queries.astype(jnp.float32), b_keys.astype(jnp.float32))
    cumul_heads = jnp.swapaxes(cumul_log, 1, 2)
    causal = jnp.arange(block_len)[:, None] >= jnp.arange(block_len)[None, :]
    log_gap = cumul_heads[:, :, :, None] - cumul_heads[:, :, None, :]
    decays = jnp.where(causal, jnp.exp(jnp.where(causal, log_gap, 0.0)), 0.0)
    weights = (decays.reshape(blocks, groups, per_group, block_len, block_len) * scores[:, :, None]).reshape(blocks, head_count, block_len, block_len).astype(jnp.bfloat16)
    intra_sum = jnp.einsum('chts,cshp->cthp', weights.astype(jnp.float32), inflow.astype(jnp.float32))
    tail_decay = jnp.exp(block_total[:, None, :] - cumul_log)
    scaled = (inflow.astype(jnp.float32) * tail_decay[..., None]).astype(jnp.bfloat16)
    states = jnp.einsum('csgkp,csgn->cgkpn', scaled.reshape(blocks, block_len, groups, per_group, channels).astype(jnp.float32), b_keys.astype(jnp.float32))
    states = states.reshape(blocks, head_count, channels, -1)
    return (cumul_log, block_total, weights, intra_sum, tail_decay, states)

def carry_chain(block_total, states, reverse):

    def advance(running, scan_item):
        fade_log, block_state = scan_item
        return (jnp.exp(fade_log)[:, None, None] * running + block_state, running)
    zero_state = jnp.zeros(states.shape[1:], jnp.float32)
    return lax.scan(advance, zero_state, (block_total, states), reverse=reverse)

def inter_forward(cumul_log, c_queries, incoming):
    blocks, block_len, head_count = cumul_log.shape
    groups = c_queries.shape[2]
    channels = incoming.shape[2]
    held_bf = incoming.astype(jnp.bfloat16).reshape(blocks, groups, head_count // groups, channels, -1)
    contracted = jnp.einsum('ctgn,cgkpn->ctgkp', c_queries.astype(jnp.float32), held_bf.astype(jnp.float32))
    return contracted.reshape(blocks, block_len, head_count, channels) * jnp.exp(cumul_log)[..., None]

def inter_backward(tail_decay, b_keys, outgoing):
    blocks, block_len, head_count = tail_decay.shape
    groups = b_keys.shape[2]
    channels = outgoing.shape[2]
    held_bf = outgoing.astype(jnp.bfloat16).reshape(blocks, groups, head_count // groups, channels, -1)
    contracted = jnp.einsum('csgn,cgkpn->csgkp', b_keys.astype(jnp.float32), held_bf.astype(jnp.float32))
    return contracted.reshape(blocks, block_len, head_count, channels) * tail_decay[..., None]

def reverse_states(cumul_log, grads, c_queries):
    blocks, block_len, head_count, channels = grads.shape
    groups = c_queries.shape[2]
    weighted = (grads * jnp.exp(cumul_log)[..., None]).astype(jnp.bfloat16)
    weighted = weighted.reshape(blocks, block_len, groups, head_count // groups, channels)
    states = jnp.einsum('ctgkp,ctgn->cgkpn', weighted.astype(jnp.float32), c_queries.astype(jnp.float32))
    return states.reshape(blocks, head_count, channels, -1)

def group_norm(values, norm_scale, groups):
    length = values.shape[0]
    grouped_view = values.reshape(length, groups, -1)
    mean_sq = lax.optimization_barrier(jnp.mean(grouped_view * grouped_view, axis=-1, keepdims=True))
    return (grouped_view * lax.rsqrt(mean_sq + eps_norm)).reshape(length, -1) * norm_scale

def mixer(padded, conv_taps, conv_offset, step_raw, step_bias, rate_log, skip_gain, norm_scale, live_mask, upstream, chain):
    length = padded.shape[0] - (CONV - 1)
    summed = conv_offset + conv_taps[0] * padded[0:length].astype(jnp.float32)
    for offset in range(1, CONV):
        summed = summed + conv_taps[offset] * padded[offset:offset + length].astype(jnp.float32)
    convolved = jax.nn.silu(summed).astype(jnp.bfloat16)
    head_count = step_raw.shape[1]
    per_group = HEADS // GROUPS
    groups_here = head_count // per_group
    grouped = convolved.reshape(length, groups_here, -1)
    inputs = grouped[:, :, :per_group * HEAD_DIM].reshape(length, head_count, HEAD_DIM)
    b_keys = grouped[:, :, per_group * HEAD_DIM:per_group * HEAD_DIM + STATE]
    c_queries = grouped[:, :, per_group * HEAD_DIM + STATE:]
    step = jax.nn.softplus(step_raw + step_bias)
    logdecay = -step * jnp.exp(rate_log)
    inflow = (step[:, :, None] * inputs.astype(jnp.float32)).astype(jnp.bfloat16)
    blocks = length // SPAN
    keys_blocks = b_keys.reshape(blocks, SPAN, groups_here, STATE)
    query_blocks = c_queries.reshape(blocks, SPAN, groups_here, STATE)
    cumul_log, block_total, weights, intra_sum, tail_decay, states = span_terms(logdecay.reshape(blocks, SPAN, head_count), inflow.reshape(blocks, SPAN, head_count, HEAD_DIM), keys_blocks, query_blocks)
    incoming = chain(block_total, states, False)
    raw = (intra_sum + inter_forward(cumul_log, query_blocks, incoming)).reshape(length, head_count, HEAD_DIM)
    raw = raw + skip_gain[:, None] * inputs.astype(jnp.float32)

    def normed(values):
        return group_norm(values.reshape(length, -1), norm_scale, groups_here)
    full_out, pullback = jax.vjp(normed, raw)
    mixed_out = (full_out * live_mask).astype(jnp.bfloat16)
    grads = pullback(upstream.astype(jnp.float32) * live_mask)[0]
    grad_blocks = grads.reshape(blocks, SPAN, head_count, HEAD_DIM)
    intra_back = jnp.einsum('chts,cthp->cshp', weights.astype(jnp.float32), grad_blocks.astype(jnp.bfloat16).astype(jnp.float32))
    outgoing = chain(block_total, reverse_states(cumul_log, grad_blocks, query_blocks), True)
    back_sum = (intra_back + inter_backward(tail_decay, keys_blocks, outgoing)).reshape(length, head_count, HEAD_DIM)
    x_grad = (skip_gain[:, None] * grads + step[:, :, None] * back_sum).reshape(length, -1).astype(jnp.bfloat16)
    return (mixed_out, x_grad)

def reference(tokens, weight, adapter_down_weight, adapter_up_weight, magnitude, step_size_weight, step_size_bias, decay_rate_log, head_skip_gain, convolution_weight, convolution_bias, grouped_norm_gain, tenant, lengths, cotangent):

    def column_norm(tenant_index):
        tenant_down_weight = lax.dynamic_index_in_dim(adapter_down_weight, tenant_index, 1, keepdims=False)
        tenant_up_weight = lax.dynamic_index_in_dim(adapter_up_weight, tenant_index, 0, keepdims=False)
        adapted = weight.astype(jnp.float32) + jnp.dot(tenant_down_weight, tenant_up_weight, preferred_element_type=jnp.float32)
        return jnp.sqrt(lax.optimization_barrier(jnp.sum(adapted * adapted, axis=0)) + eps_column)
    colnorm = lax.map(column_norm, jnp.arange(TENANT_COUNT, dtype=jnp.int32))

    def plain_chain(block_total, states, reverse):
        return carry_chain(block_total, states, reverse)[1]

    def one_sequence(scan_item):
        seq_tokens, tenant_index, length, upstream = scan_item
        tenant_down_weight = lax.dynamic_index_in_dim(adapter_down_weight, tenant_index, 1, keepdims=False)
        tenant_up_weight = lax.dynamic_index_in_dim(adapter_up_weight, tenant_index, 0, keepdims=False)
        mag_own = lax.dynamic_index_in_dim(magnitude, tenant_index, 0, keepdims=False)
        norm_own = lax.dynamic_index_in_dim(colnorm, tenant_index, 0, keepdims=False)
        base_proj = jnp.dot(seq_tokens, weight, preferred_element_type=jnp.float32)
        low_rank = jnp.dot(seq_tokens, tenant_down_weight, preferred_element_type=jnp.float32).astype(jnp.bfloat16)
        projected = ((base_proj + jnp.dot(low_rank, tenant_up_weight, preferred_element_type=jnp.float32)) * (mag_own / norm_own)).astype(jnp.bfloat16)
        padded = jnp.concatenate([jnp.zeros((CONV - 1, projected.shape[1]), jnp.bfloat16), projected], axis=0)
        step_raw = jnp.dot(seq_tokens, step_size_weight, preferred_element_type=jnp.float32)
        live_mask = (jnp.arange(seq_tokens.shape[0], dtype=jnp.int32) < length)[:, None]
        return mixer(padded, convolution_weight, convolution_bias, step_raw, step_size_bias, decay_rate_log, head_skip_gain, grouped_norm_gain, live_mask, upstream, plain_chain)
    mixed, x_grad = lax.map(one_sequence, (tokens, tenant, lengths, cotangent))
    return (mixed, x_grad)
```

```python
import jax
import jax.numpy as jnp
from jax import lax
from jax.experimental import pallas as pl
from jax.experimental.pallas import tpu as pltpu
from jax.sharding import Mesh, PartitionSpec as P

HEADS = 128
HEAD_DIM = 64
GROUPS = 8
STATE = 128
CONV = 4
SPAN = 128
RING = 4
ROWS = 64
WIDTH = 4096
LEN = 256
TENANTS = 4
RANK = 16
HALF = 640
GROUP_COLS = 1280
GROUP_CHANNELS = 1024
GROUP_HEADS = 16
EXTRA = 128
FIRST = HALF + EXTRA
PIECE = FIRST // 2
NORM_ROWS = 16

eps_norm = 1e-05
eps_column = 1e-06

f32 = jnp.float32
bf16 = jnp.bfloat16


def shift(v, axis, by):
    return lax.ppermute(v, axis, [(i, (i + by) % RING) for i in range(RING)])


def swap(v, axis, mask):
    return lax.ppermute(v, axis, [(i, i ^ mask) for i in range(RING)])


def cross(v):
    return lax.ppermute(v, "seq", [(0, 1), (1, 0)])


def pick(v, index):
    return lax.dynamic_index_in_dim(v, index, 0, keepdims=False)


def place_order(own, right, opposite, left, x):
    twice = jnp.stack([own, right, opposite, left, own, right, opposite, left])
    return lax.dynamic_slice_in_dim(twice, (RING - x) % RING, RING, 0)


def token_copies(tok_refs, tokens, sem, c, k, width):
    cols = pl.ds(k * width, width)
    for part, place in ((0, c), (1, 1 - c)):
        base = pl.multiple_of(place * SPAN, SPAN)
        own, left, right, opp1, opp2 = tok_refs[5 * part : 5 * part + 5]
        for which, (ref, rows, extra) in enumerate(
            ((own, SPAN, 0), (left, SPAN, LEN), (right, SPAN, 2 * LEN), (opp1, 64, 3 * LEN), (opp2, 64, 3 * LEN + 64))
        ):
            pltpu.make_async_copy(
                ref.at[:, cols], tokens.at[pl.ds(base + extra, rows), cols], sem
            ).start()


def wait_all(ref, sem):
    pltpu.make_async_copy(ref, ref, sem).wait()


def bits(own, at):
    gap = own ^ at
    far = gap >> 1
    return (gap ^ far) & 1, far


def project_first(meta, *refs):
    tok_refs = refs[:10]
    held = refs[10:14]
    came = refs[14:18]
    up_ref, mag_ref = refs[18:20]
    outs = refs[20:24]
    low_out, step_out, scale_out = refs[24:27]
    tokens, panel, norms, acc, tok_sem, panel_sem, norm_sem = refs[27:]
    c, x, y, z = meta[0], meta[1], meta[2], meta[3]
    width = WIDTH // RING

    def fetch(k):
        token_copies(tok_refs, tokens, tok_sem.at[k], c, k, width)
        zn, zf = bits(z, k)
        for yt in range(RING):
            yn, yf = bits(y, yt)
            at = (k * RING + yt) * 256
            orders = (
                (yn + 2 * zn + 4 * yf, zf, 0, 0),
                (yn + 2 * zn + 4 * zf, yf, 0, PIECE),
                (zf + 2 * yf + 4 * yn, zn, 128, 0),
                (zf + 2 * yf + 4 * zn, yn, 128, PIECE),
            )
            for i, (entry, last, row, col) in enumerate(orders):

                def go(ref, entry=entry, row=row, col=col, at=at, i=i, yt=yt):
                    pltpu.make_async_copy(
                        ref.at[entry, pl.ds(0, 128), :],
                        panel.at[pl.ds(at + row, 128), pl.ds(col, PIECE)],
                        panel_sem.at[k],
                    ).start()
                    if i < 2:
                        pltpu.make_async_copy(
                            ref.at[entry, pl.ds(128, NORM_ROWS), :],
                            norms.at[k * RING + yt, :, pl.ds(col, PIECE)],
                            norm_sem,
                        ).start()

                @pl.when(last == 0)
                def _(i=i, go=go):
                    go(held[i])

                @pl.when(last == 1)
                def _(i=i, go=go):
                    go(came[i])

    for k in range(RING):
        fetch(k)
    for k in range(RING):
        cols = pl.ds(k * width, width)
        wait_all(tokens.at[:, cols], tok_sem.at[k])
        wait_all(panel.at[cols, :], panel_sem.at[k])

        def tile(m, _, k=k, cols=cols):
            rows = pl.ds(pl.multiple_of(m * 512, 512), 512)
            new = jnp.dot(tokens[rows, cols], panel[cols, :], preferred_element_type=f32)
            if k == 0:
                acc[rows, :] = new
            else:
                acc[rows, :] += new
            return 0

        lax.fori_loop(0, 2, tile, 0)
    wait_all(norms, norm_sem)
    total = jnp.sum(norms[...].astype(f32), axis=0)
    first = total[0:4, :HALF] + total[4:8, :HALF]
    second = total[8:12, :HALF] + total[12:16, :HALF]
    scale1 = mag_ref[:, :HALF] / jnp.sqrt(first + eps_column)
    scale2 = mag_ref[:, HALF:] / jnp.sqrt(second + eps_column)
    scale_out[...] = scale2
    step_out[...] = acc[0:LEN, HALF + 64 :]
    lane_tenant = lax.broadcasted_iota(jnp.int32, (LEN, 64), 1) // RANK
    for s in range(RING):
        tenant = meta[4 + s]
        rows = pl.ds(s * LEN, LEN)
        low = jnp.where(lane_tenant == tenant, acc[rows, HALF : HALF + 64], 0.0).astype(bf16)
        low_out[s] = low
        adapted = acc[rows, :HALF] + jnp.dot(low, up_ref[...], preferred_element_type=f32)
        outs[s][...] = (adapted * tenant_row(scale1, tenant)).astype(bf16)


def tenant_row(table, tenant):
    row = table[0:1]
    for k in range(1, TENANTS):
        row = jnp.where(tenant == k, table[k : k + 1], row)
    return row


def project_second(meta, *refs):
    tok_refs = refs[:10]
    weight_ref, low_ref, scale_ref, up_ref = refs[10:14]
    outs = refs[14:18]
    tokens, panel, acc, tok_sem, panel_sem = refs[18:]
    c = meta[0]
    width = WIDTH // RING
    for k in range(RING):
        cols = pl.ds(k * width, width)
        token_copies(tok_refs, tokens, tok_sem.at[k], c, k, width)
        pltpu.make_async_copy(weight_ref.at[cols, :], panel.at[cols, :], panel_sem.at[k]).start()
    for k in range(RING):
        cols = pl.ds(k * width, width)
        wait_all(tokens.at[:, cols], tok_sem.at[k])
        wait_all(panel.at[cols, :], panel_sem.at[k])

        def tile(m, _, k=k, cols=cols):
            rows = pl.ds(pl.multiple_of(m * 512, 512), 512)
            new = jnp.dot(tokens[rows, cols], panel[cols, :], preferred_element_type=f32)
            if k == 0:
                acc[rows, :] = new
            else:
                acc[rows, :] += new
            return 0

        lax.fori_loop(0, 2, tile, 0)
    for s in range(RING):
        tenant = meta[4 + s]
        rows = pl.ds(s * LEN, LEN)
        adapted = acc[rows, :] + jnp.dot(low_ref[s], up_ref[...], preferred_element_type=f32)
        outs[s][...] = (adapted * tenant_row(scale_ref[...], tenant)).astype(bf16)


def any_specs(n):
    return [pl.BlockSpec(memory_space=pl.ANY)] * n


def vmem_specs(n):
    return [pl.BlockSpec(memory_space=pltpu.VMEM)] * n


def run_first(meta, tok, held, came, up, mag):
    rows = RING * LEN
    out = jax.ShapeDtypeStruct((LEN, HALF), bf16)
    return pl.pallas_call(
        project_first,
        in_specs=[pl.BlockSpec(memory_space=pltpu.SMEM)] + any_specs(18) + vmem_specs(2),
        out_specs=vmem_specs(7),
        out_shape=[
            out,
            out,
            out,
            out,
            jax.ShapeDtypeStruct((RING, LEN, 64), bf16),
            jax.ShapeDtypeStruct((LEN, 64), f32),
            jax.ShapeDtypeStruct((TENANTS, HALF), f32),
        ],
        scratch_shapes=[
            pltpu.VMEM((rows, WIDTH), bf16),
            pltpu.VMEM((WIDTH, FIRST), bf16),
            pltpu.VMEM((16, NORM_ROWS, FIRST), bf16),
            pltpu.VMEM((rows, FIRST), f32),
            pltpu.SemaphoreType.DMA((RING,)),
            pltpu.SemaphoreType.DMA((RING,)),
            pltpu.SemaphoreType.DMA,
        ],
        compiler_params=pltpu.CompilerParams(vmem_limit_bytes=40 << 20),
        cost_estimate=pl.CostEstimate(
            flops=2 * rows * WIDTH * FIRST, bytes_accessed=16 << 20, transcendentals=0
        ),
        name="project_first",
    )(meta, *tok, *held, *came, up, mag)


def run_second(meta, tok, weight, low, scale, up):
    rows = RING * LEN
    out = jax.ShapeDtypeStruct((LEN, HALF), bf16)
    return pl.pallas_call(
        project_second,
        in_specs=[pl.BlockSpec(memory_space=pltpu.SMEM)] + any_specs(11) + vmem_specs(3),
        out_specs=vmem_specs(4),
        out_shape=[out, out, out, out],
        scratch_shapes=[
            pltpu.VMEM((rows, WIDTH), bf16),
            pltpu.VMEM((WIDTH, HALF), bf16),
            pltpu.VMEM((rows, HALF), f32),
            pltpu.SemaphoreType.DMA((RING,)),
            pltpu.SemaphoreType.DMA((RING,)),
        ],
        compiler_params=pltpu.CompilerParams(vmem_limit_bytes=40 << 20),
        cost_estimate=pl.CostEstimate(
            flops=2 * rows * WIDTH * HALF, bytes_accessed=16 << 20, transcendentals=0
        ),
        name="project_second",
    )(meta, *tok, weight, low, scale, up)


def contract_first(a, b):
    return lax.dot_general(a, b, (((0,), (0,)), ((), ())), preferred_element_type=f32)


def contract_last(a, b):
    return lax.dot_general(a, b, (((1,), (1,)), ((), ())), preferred_element_type=f32)


def scan_kernel(aliased, meta, *refs):
    p1, p2, taps, offset, gain, skip, step_ref, cumul_ref, cumul_t_ref, cot_own, cot_other = refs[:11]
    refs = refs[11 + aliased :]
    mixed_ref, grad_ref, send_ref = refs[:3]
    padded, conv, raws, grads, incoming, outgoing, mixed_all, x_all = refs[3:]
    c, length = meta[0], meta[3]
    pairs = GROUP_HEADS // 2
    padded[0:8, :] = jnp.zeros((8, GROUP_COLS), f32)
    padded[8:, :HALF] = p1[...].astype(f32)
    padded[8:, HALF:] = p2[...].astype(f32)
    summed = offset[...] + taps[0:1, :] * padded[5 : 5 + LEN, :]
    for i in range(1, CONV):
        summed = summed + taps[i : i + 1, :] * padded[5 + i : 5 + i + LEN, :]
    conv[...] = (summed / (1.0 + jnp.exp(-summed))).astype(bf16)
    causal = lax.broadcasted_iota(jnp.int32, (SPAN, SPAN), 0) >= lax.broadcasted_iota(
        jnp.int32, (SPAN, SPAN), 1
    )
    anti = lax.broadcasted_iota(jnp.int32, (SPAN, SPAN), 0) <= lax.broadcasted_iota(
        jnp.int32, (SPAN, SPAN), 1
    )
    low_lane = lax.broadcasted_iota(jnp.int32, (SPAN, SPAN), 1) < HEAD_DIM

    def spread(ref, rows, head):
        return jnp.broadcast_to(ref[0, rows, head : head + 1], (SPAN, SPAN))

    def stacked(values):
        zero = jnp.zeros_like(values)
        return jnp.concatenate(
            [jnp.where(low_lane, values, zero), jnp.where(low_lane, zero, values)], axis=0
        )

    for block in range(LEN // SPAN):
        rows = slice(block * SPAN, (block + 1) * SPAN)
        keys = conv[rows, GROUP_CHANNELS : GROUP_CHANNELS + STATE]
        queries = conv[rows, GROUP_CHANNELS + STATE :]
        scores = jnp.where(causal, contract_last(queries, keys), 0.0)
        squares = jnp.zeros((SPAN, SPAN), f32)
        for q in range(pairs):
            lanes = slice(q * SPAN, (q + 1) * SPAN)
            values = conv[rows, lanes].astype(f32)
            level = [spread(cumul_ref, rows, 2 * q + i) for i in range(2)]
            mix = [
                (
                    jnp.exp(jnp.minimum(level[i] - cumul_t_ref[0, 2 * q + i : 2 * q + i + 1, rows], 0.0))
                    * scores
                ).astype(bf16)
                for i in range(2)
            ]
            step = jnp.where(low_lane, spread(step_ref, rows, 2 * q), spread(step_ref, rows, 2 * q + 1))
            inflow = (step * values).astype(bf16)
            raw = jnp.dot(
                jnp.concatenate(mix, axis=1), stacked(inflow), preferred_element_type=f32
            )
            both = jnp.where(low_lane, level[0], level[1])
            if block == 0:
                tail = jnp.exp(both[SPAN - 1 :, :] - both)
                scaled = (inflow.astype(f32) * tail).astype(bf16)
                incoming[:, lanes] = contract_first(keys, scaled).astype(bf16)
            else:
                raw = raw + jnp.dot(
                    queries, incoming[:, lanes], preferred_element_type=f32
                ) * jnp.exp(both)
            raw = raw + skip[:, lanes] * values
            raws[rows, lanes] = raw
            squares = squares + raw * raw
        mean_sq = jnp.sum(squares, axis=1, keepdims=True) / GROUP_CHANNELS
        inverse = lax.rsqrt(mean_sq + eps_norm)
        at = block * SPAN + lax.broadcasted_iota(jnp.int32, (SPAN, 1), 0)
        live = jnp.where(at < length, 1.0, 0.0)
        upstream = jnp.where(c == block, cot_own[...], cot_other[...]).astype(f32) * live
        raw = raws[rows, :]
        scaled_up = upstream * gain[...]
        mixed_all[rows, :] = ((gain[...] * raw) * (inverse * live)).astype(bf16)
        along = jnp.sum(scaled_up * raw, axis=1, keepdims=True) / GROUP_CHANNELS
        grads[rows, :] = scaled_up * inverse - raw * (along * inverse * inverse * inverse)

    for block in reversed(range(LEN // SPAN)):
        rows = slice(block * SPAN, (block + 1) * SPAN)
        keys = conv[rows, GROUP_CHANNELS : GROUP_CHANNELS + STATE]
        queries = conv[rows, GROUP_CHANNELS + STATE :]
        scores = jnp.where(anti, contract_last(keys, queries), 0.0)
        for q in range(pairs):
            lanes = slice(q * SPAN, (q + 1) * SPAN)
            level = [spread(cumul_ref, rows, 2 * q + i) for i in range(2)]
            mix = [
                (
                    jnp.exp(jnp.minimum(cumul_t_ref[0, 2 * q + i : 2 * q + i + 1, rows] - level[i], 0.0))
                    * scores
                ).astype(bf16)
                for i in range(2)
            ]
            step = jnp.where(low_lane, spread(step_ref, rows, 2 * q), spread(step_ref, rows, 2 * q + 1))
            grad = grads[rows, lanes]
            back = jnp.dot(
                jnp.concatenate(mix, axis=1), stacked(grad.astype(bf16)), preferred_element_type=f32
            )
            both = jnp.where(low_lane, level[0], level[1])
            if block == 1:
                weighted = (grad * jnp.exp(both)).astype(bf16)
                outgoing[:, lanes] = contract_first(queries, weighted).astype(bf16)
            else:
                tail = jnp.exp(both[SPAN - 1 :, :] - both)
                back = back + jnp.dot(keys, outgoing[:, lanes], preferred_element_type=f32) * tail
            x_all[rows, lanes] = (skip[:, lanes] * grad + step * back).astype(bf16)

    mine = pl.ds(pl.multiple_of(c * SPAN, SPAN), SPAN)
    others = pl.ds(pl.multiple_of((1 - c) * SPAN, SPAN), SPAN)
    mixed_ref[...] = mixed_all[mine, :]
    grad_ref[...] = x_all[mine, :]
    send_ref[0] = mixed_all[others, :]
    send_ref[1] = x_all[others, :]


def run_scan(meta, p1, p2, shared, cot, cot_other, totals):
    taps, offset, gain, skip, step, cumul, cumul_t = shared
    full = pl.BlockSpec((LEN, HALF), lambda i, m: (0, 0))
    out_full = jax.ShapeDtypeStruct((SPAN, GROUPS * GROUP_CHANNELS), bf16)
    aliased = 0 if totals is None else 2
    extra = () if totals is None else tuple(totals)

    def kernel(*refs):
        scan_kernel(aliased, *refs)

    return pl.pallas_call(
        kernel,
        grid_spec=pltpu.PrefetchScalarGridSpec(
            num_scalar_prefetch=1,
            grid=(1,),
            in_specs=[
                full,
                full,
                pl.BlockSpec((CONV, GROUP_COLS), lambda i, m: (0, m[2])),
                pl.BlockSpec((1, GROUP_COLS), lambda i, m: (0, m[2])),
                pl.BlockSpec((1, GROUP_CHANNELS), lambda i, m: (0, m[2])),
                pl.BlockSpec((1, GROUP_CHANNELS), lambda i, m: (0, m[2])),
                pl.BlockSpec((1, LEN, GROUP_HEADS), lambda i, m: (m[1], 0, 0)),
                pl.BlockSpec((1, LEN, GROUP_HEADS), lambda i, m: (m[1], 0, 0)),
                pl.BlockSpec((1, GROUP_HEADS, LEN), lambda i, m: (m[1], 0, 0)),
                pl.BlockSpec((SPAN, GROUP_CHANNELS), lambda i, m: (0, m[2])),
                pl.BlockSpec((SPAN, GROUP_CHANNELS), lambda i, m: (0, m[1])),
            ]
            + any_specs(aliased),
            out_specs=[
                pl.BlockSpec((SPAN, GROUP_CHANNELS), lambda i, m: (0, m[2])),
                pl.BlockSpec((SPAN, GROUP_CHANNELS), lambda i, m: (0, m[2])),
                pl.BlockSpec((2, SPAN, GROUP_CHANNELS), lambda i, m: (0, 0, 0)),
            ],
            scratch_shapes=[
                pltpu.VMEM((LEN + 8, GROUP_COLS), f32),
                pltpu.VMEM((LEN, GROUP_COLS), bf16),
                pltpu.VMEM((LEN, GROUP_CHANNELS), f32),
                pltpu.VMEM((LEN, GROUP_CHANNELS), f32),
                pltpu.VMEM((STATE, GROUP_CHANNELS), bf16),
                pltpu.VMEM((STATE, GROUP_CHANNELS), bf16),
                pltpu.VMEM((LEN, GROUP_CHANNELS), bf16),
                pltpu.VMEM((LEN, GROUP_CHANNELS), bf16),
            ],
        ),
        out_shape=[out_full, out_full, jax.ShapeDtypeStruct((2, SPAN, GROUP_CHANNELS), bf16)],
        input_output_aliases={} if totals is None else {12: 0, 13: 1},
        compiler_params=pltpu.CompilerParams(vmem_limit_bytes=32 << 20),
        cost_estimate=pl.CostEstimate(flops=1 << 30, bytes_accessed=4 << 20, transcendentals=2 << 20),
        name="scan_group",
    )(meta, p1, p2, taps, offset, gain, skip, step, cumul, cumul_t, cot, cot_other, *extra)


def split_sum(values):
    high = lax.reduce_precision(values, 8, 7)
    return high.astype(bf16), (values - high).astype(bf16)


def norm_rows(sums):
    high, low = split_sum(sums)
    return jnp.concatenate(
        [high[..., :HALF], low[..., :HALF], high[..., HALF:], low[..., HALF:]], axis=-2
    )


def per_device(
    tokens,
    weight,
    adapter_down_weight,
    adapter_up_weight,
    magnitude,
    step_size_weight,
    step_size_bias,
    decay_rate_log,
    head_skip_gain,
    convolution_weight,
    convolution_bias,
    grouped_norm_gain,
    tenant,
    lengths,
    cotangent,
):
    c, x, y, z = (lax.axis_index(name) for name in ("seq", "x", "y", "z"))
    own_tokens = tokens[0]
    upstream = cotangent[0]
    by_chip = jnp.swapaxes(weight.reshape(ROWS, RING, GROUP_COLS), 0, 1)

    second = [pick(by_chip[:, :, HALF:], (x + d) % RING) for d in range(RING)]
    second = place_order(
        second[0],
        shift(second[3], "x", -1),
        shift(second[2], "x", 2),
        shift(second[1], "x", 1),
        x,
    )
    second_panel = lax.all_gather(
        second.reshape(RING * ROWS, HALF), ("z", "y"), axis=0, tiled=True
    )

    adapted = weight.astype(f32)[None] + jnp.einsum(
        "gbc,bco->bgo", adapter_down_weight, adapter_up_weight, preferred_element_type=f32
    )
    sums = jnp.sum(adapted * adapted, axis=1).reshape(TENANTS, RING, GROUP_COLS)
    norm_part = norm_rows(jnp.swapaxes(sums, 0, 1))
    tenant_mark = jnp.broadcast_to(tenant[0].astype(bf16), (RING, NORM_ROWS, EXTRA))
    heads_here = HEADS // 2
    extras = jnp.concatenate(
        [
            adapter_down_weight.reshape(ROWS, TENANTS * RANK),
            lax.dynamic_slice_in_dim(step_size_weight, c * heads_here, heads_here, 1),
        ],
        axis=1,
    )
    first_all = jnp.concatenate(
        [
            jnp.concatenate(
                [by_chip[:, :, :HALF], jnp.broadcast_to(extras, (RING, ROWS, EXTRA))], axis=2
            ),
            jnp.concatenate([norm_part, tenant_mark], axis=2),
        ],
        axis=1,
    )
    first = [pick(first_all, (x + d) % RING) for d in range(RING)]
    first_from = [
        first[0],
        shift(first[3], "x", -1),
        shift(first[2], "x", 2),
        shift(first[1], "x", 1),
    ]
    tenants = [tenant[0]] + [
        first_from[i][ROWS, HALF].astype(jnp.int32) for i in (3, 1, 2)
    ]
    rows = place_order(*[block[:ROWS] for block in first_from], x)
    marks = sum(block[ROWS:, :HALF].astype(f32) for block in first_from)
    sums = jnp.concatenate([marks[0:4] + marks[4:8], marks[8:12] + marks[12:16]], axis=1)
    marks = jnp.pad(norm_rows(sums), ((0, 0), (0, EXTRA)))
    a = jnp.concatenate([rows[:2].reshape(2 * ROWS, FIRST), marks], axis=0)[None]
    b = rows[2:].reshape(1, 2 * ROWS, FIRST)
    a = jnp.concatenate([a, swap(a, "y", 1)], axis=0)
    b = jnp.concatenate([b, swap(b, "z", 3)], axis=0)
    a = jnp.concatenate([a, swap(a, "z", 1)], axis=0)
    b = jnp.concatenate([b, swap(b, "y", 3)], axis=0)
    parts = [a[:, :, :PIECE], a[:, :, PIECE:], b[:, :, :PIECE], b[:, :, PIECE:]]
    third = (("y", 3), ("z", 3), ("y", 1), ("z", 1))
    fourth = (("z", 3), ("y", 3), ("z", 1), ("y", 1))
    held = [
        jnp.concatenate([part, swap(part, *how)], axis=0) for part, how in zip(parts, third)
    ]
    came = [swap(part, *how) for part, how in zip(held, fourth)]

    left = shift(own_tokens, "x", 1)
    right = shift(own_tokens, "x", -1)
    half = SPAN // 2
    pieces = [own_tokens, left, right, shift(left[:half], "x", 1), shift(right[half:], "x", -1)]
    tok = pieces + [cross(piece) for piece in pieces]

    per_core = GROUPS // 2 * GROUP_CHANNELS
    cot_other = cross(lax.dynamic_slice_in_dim(upstream, (1 - c) * per_core, per_core, 1))

    up = lax.dynamic_slice_in_dim(
        adapter_up_weight.reshape(TENANTS * RANK, RING * GROUP_COLS), x * GROUP_COLS, GROUP_COLS, 1
    )
    mag = lax.dynamic_slice_in_dim(magnitude, x * GROUP_COLS, GROUP_COLS, 1)
    meta = jnp.stack([c, x, y, z] + tenants).astype(jnp.int32)
    *front, low, step_raw, scale = run_first(meta, tok, held, came, up[:, :HALF], mag)
    back = run_second(meta, tok, second_panel, low, scale, up[:, HALF:])

    def own_heads(v):
        return lax.dynamic_slice_in_dim(v, c * heads_here, heads_here, 0)

    step = jax.nn.softplus(step_raw + own_heads(step_size_bias))
    logdecay = (-step * jnp.exp(own_heads(decay_rate_log))).reshape(2, SPAN, heads_here)
    ones = jnp.tril(jnp.ones((SPAN, SPAN), f32))
    cumul = jnp.einsum(
        "ts,bsh->bth", ones, logdecay, precision=lax.Precision.HIGHEST, preferred_element_type=f32
    ).reshape(LEN, RING, GROUP_HEADS)
    shared = (
        convolution_weight,
        convolution_bias[None],
        grouped_norm_gain[None],
        jnp.repeat(head_skip_gain, HEAD_DIM)[None],
        jnp.swapaxes(step.reshape(LEN, RING, GROUP_HEADS), 0, 1),
        jnp.swapaxes(cumul, 0, 1),
        jnp.transpose(cumul, (1, 2, 0)),
    )

    def returned(values):
        own, to_left, to_right, to_opposite = values
        return [own, shift(to_left, "x", -1), shift(to_right, "x", 1), shift(to_opposite, "x", 2)]

    front, back = returned(front), returned(back)
    totals = None
    sends = []
    for i, d in ((0, 0), (1, 1), (2, 3), (3, 2)):
        group = (x + d) % RING
        scan_meta = jnp.stack([c, group, RING * c + group, lengths[0]]).astype(jnp.int32)
        *totals, send = run_scan(
            scan_meta, front[i], back[i], shared, upstream, cot_other, totals
        )
        sends.append((group, cross(send)))
    mixed, x_grad = totals
    for group, got in sends:
        at = (RING * (1 - c) + group) * GROUP_CHANNELS
        mixed = lax.dynamic_update_slice_in_dim(mixed, got[0], at, 1)
        x_grad = lax.dynamic_update_slice_in_dim(x_grad, got[1], at, 1)
    return (mixed[None], x_grad[None])


def solution(mesh):
    chips = Mesh(mesh.devices.reshape(2, RING, RING, RING), ("seq", "z", "y", "x"))
    fsdp = ("z", "y", "x")
    return jax.shard_map(
        per_device,
        mesh=chips,
        in_specs=(
            P(fsdp, "seq", None),
            P(fsdp, "seq"),
            P(fsdp, None, None),
            P(None, None, "seq"),
            P(None, "seq"),
            P(fsdp, None),
            P(),
            P(),
            P(),
            P(),
            P(),
            P(),
            P(fsdp),
            P(fsdp),
            P(fsdp, "seq", None),
        ),
        out_specs=(P(fsdp, "seq", None), P(fsdp, "seq", None)),
        check_vma=False,
    )
```

```python
import jax
import jax.numpy as jnp
from jax import lax
from jax.experimental import pallas as pl
from jax.experimental.pallas import tpu as pltpu
from jax.sharding import Mesh, PartitionSpec as P

HEADS = 128
HEAD_DIM = 64
GROUPS = 8
STATE = 128
CONV = 4
SPAN = 128
RING = 4
ROWS = 64
WIDTH = 4096
LEN = 256
TENANTS = 4
RANK = 16
FRONT = 512
GROUP_COLS = 1280
BACK = GROUP_COLS - FRONT
GROUP_CHANNELS = 1024
GROUP_HEADS = 16
EXTRA = 128
PANEL = FRONT + EXTRA
NORM_ROWS = 16
DEPTH = 256

eps_norm = 1e-05
eps_column = 1e-06

f32 = jnp.float32
bf16 = jnp.bfloat16


def shift(v, axis, by):
    return lax.ppermute(v, axis, [(i, (i + by) % RING) for i in range(RING)])


def turn(v, axis, by):
    steps = (by, -by)
    return lax.ppermute(
        v,
        ("seq", axis),
        [(k * RING + i, k * RING + (i + steps[k]) % RING) for k in range(2) for i in range(RING)],
    )


def swap(v, axis, near):
    masks = (1, 3) if near else (3, 1)
    return lax.ppermute(
        v,
        ("seq", axis),
        [(k * RING + i, k * RING + (i ^ masks[k])) for k in range(2) for i in range(RING)],
    )


def cross(v):
    return lax.ppermute(v, "seq", [(0, 1), (1, 0)])


def pick(v, index):
    return lax.dynamic_index_in_dim(v, index, 0, keepdims=False)


def place_order(own, right, opposite, left, x):
    twice = jnp.stack([own, right, opposite, left, own, right, opposite, left])
    return lax.dynamic_slice_in_dim(twice, (RING - x) % RING, RING, 0)


def wait_all(ref, sem):
    pltpu.make_async_copy(ref, ref, sem).wait()


def bits(own, at, c):
    gap = own ^ at
    far = gap >> 1
    near = (gap ^ far) & 1
    return jnp.where(c == 0, near, far), jnp.where(c == 0, far, near)


def half_ranges(meta, order, came):
    c, y, z = meta[0], meta[2], meta[3]
    near, far = 1 + 2 * c, 3 - 2 * c
    split = z if order == "yz" else y
    places = [split ^ (came * far) ^ (i * near) for i in range(2)]
    if order == "yz":
        width = RING * DEPTH
        starts = [place * width for place in places]
    else:
        width = DEPTH
        starts = [(at * RING + place) * width for at in range(RING) for place in places]
    return [pl.multiple_of(start, DEPTH) for start in starts], width


def half_copies(meta, order, panel_refs, panel, sem):
    other = meta[2] if order == "yz" else meta[3]
    for at in range(RING):
        first, second = bits(other, at, meta[0])
        for i in range(2):
            slot = i * RING + at if order == "yz" else at * 2 + i
            for half in range(2):

                @pl.when(second == half)
                def _(i=i, half=half, first=first, slot=slot):
                    pltpu.make_async_copy(
                        panel_refs[half].at[first + 2 * i, pl.ds(0, DEPTH), :], panel.at[slot], sem
                    ).start()


def piece_copies(tok_refs, pieces, sem):
    for i, ref in enumerate(tok_refs):
        pltpu.make_async_copy(ref, pieces.at[i], sem.at[i]).start()


def half_products(meta, order, came, pieces, piece_sem, panel, emit):
    c = meta[0]
    starts, width = half_ranges(meta, order, came)
    for source, place in ((0, c), (1, 1 - c)):
        sequences = (0, 1 + place, 2 - place, 3)
        for i, sequence in enumerate(sequences):
            at = 4 * source + i
            if piece_sem is not None:
                wait_all(pieces.at[at], piece_sem.at[at])
            rows = pl.ds(pl.multiple_of(sequence * LEN + place * SPAN, SPAN), SPAN)
            piece = jnp.concatenate([pieces[at, :, pl.ds(start, width)] for start in starts], axis=1)
            whole = panel[...].reshape(WIDTH // 2, panel.shape[-1])
            emit(rows, jnp.dot(piece, whole, preferred_element_type=f32))


def project_held(meta, *refs):
    tok_refs, front_ref, back_ref = refs[:8], refs[8:10], refs[10:12]
    front_out, back_out, front_panel, back_panel, pieces, sem, piece_sem = refs[12:]
    parts = (("yz", front_ref, front_panel, front_out), ("zy", back_ref, back_panel, back_out))
    for i, (order, ref, panel, _) in enumerate(parts):
        half_copies(meta, order, ref, panel, sem.at[i])
        if i == 0:
            piece_copies(tok_refs, pieces, piece_sem)
    for i, (order, _, panel, out) in enumerate(parts):
        wait_all(panel, sem.at[i])

        def emit(rows, product, out=out):
            out[rows, :] = product

        half_products(meta, order, 0, pieces, piece_sem if i == 0 else None, panel, emit)


def project_came(meta, *refs):
    tok_refs, front_held, front_ref, back_ref = refs[:8], refs[8:10], refs[10:12], refs[12:14]
    up_ref, mag_ref, bias_ref, rate_ref, front_base, back_base = refs[14:20]
    outs = refs[20:24]
    step_out, cumul_out, cumul_t_out = refs[24:27]
    front_panel, back_panel, pieces, front_acc, back_acc, ready, norms = refs[27:34]
    sem, piece_sem, ready_sem, norm_sem = refs[34:]
    c = meta[0]
    for i, ref in enumerate((*front_held, *front_ref)):
        pltpu.make_async_copy(
            ref.at[:, pl.ds(DEPTH, NORM_ROWS), :], norms.at[pl.ds(4 * i, 4)], norm_sem
        ).start()
    parts = (
        ("yz", front_ref, front_panel, front_base, front_acc),
        ("zy", back_ref, back_panel, back_base, back_acc),
    )
    for i, (order, ref, panel, _, _) in enumerate(parts):
        half_copies(meta, order, ref, panel, sem.at[i])
        if i == 0:
            piece_copies(tok_refs, pieces, piece_sem)
    wait_all(norms, norm_sem)
    total = jnp.sum(norms[...].astype(f32), axis=0)
    squares = [total[8 * i : 8 * i + 4] + total[8 * i + 4 : 8 * i + 8] for i in range(2)]
    squares = jnp.concatenate(squares, axis=1)
    scale = mag_ref[...] / jnp.sqrt(squares + eps_column)
    up = padded_up(up_ref)
    for i, (order, _, panel, base, acc) in enumerate(parts):
        wait_all(panel, sem.at[i])

        def emit(rows, product, base=base, acc=acc):
            acc[rows, :] = base[rows, :] + product

        half_products(meta, order, 1, pieces, piece_sem if i == 0 else None, panel, emit)
    lane_tenant = lax.broadcasted_iota(jnp.int32, (LEN, EXTRA), 1) // RANK - RING
    for s in (1, 2, 3, 0):
        tenant = meta[4 + s]
        rows = pl.ds(s * LEN, LEN)
        low = jnp.where(lane_tenant == tenant, front_acc[rows, FRONT:], 0.0).astype(bf16)
        for acc, cols in ((front_acc, slice(0, FRONT)), (back_acc, slice(FRONT, GROUP_COLS))):
            result = acc[rows, : cols.stop - cols.start] + jnp.dot(
                low, up[:, cols], preferred_element_type=f32
            )
            ready[s, :, cols] = (result * tenant_row(scale[:, cols], tenant)).astype(bf16)
        pltpu.make_async_copy(ready.at[s], outs[s], ready_sem.at[s]).start()
    heads_here = HEADS // 2
    bias = jnp.where(c == 0, bias_ref[:, :heads_here], bias_ref[:, heads_here:])
    rate = jnp.where(c == 0, rate_ref[:, :heads_here], rate_ref[:, heads_here:])
    raw = front_acc[0:LEN, FRONT : FRONT + heads_here] + bias
    step = jnp.maximum(raw, 0.0) + jnp.log1p(jnp.exp(-jnp.abs(raw)))
    logdecay = -step * jnp.exp(rate)
    ones = jnp.where(
        lax.broadcasted_iota(jnp.int32, (SPAN, SPAN), 0)
        >= lax.broadcasted_iota(jnp.int32, (SPAN, SPAN), 1),
        1.0,
        0.0,
    )
    for block in range(LEN // SPAN):
        rows = slice(block * SPAN, (block + 1) * SPAN)
        cumul = jnp.dot(
            ones, logdecay[rows], precision=lax.Precision.HIGHEST, preferred_element_type=f32
        )
        cumul_t = cumul.T
        for g in range(RING):
            heads = slice(g * GROUP_HEADS, (g + 1) * GROUP_HEADS)
            step_out[g, rows, :] = step[rows, heads]
            cumul_out[g, rows, :] = cumul[:, heads]
            cumul_t_out[g, :, rows] = cumul_t[heads, :]
    for s in range(RING):
        pltpu.make_async_copy(ready.at[s], outs[s], ready_sem.at[s]).wait()


def padded_up(up_ref):
    return jnp.concatenate([jnp.zeros((EXTRA - TENANTS * RANK, GROUP_COLS), bf16), up_ref[...]], axis=0)


def tenant_row(table, tenant):
    row = table[0:1]
    for k in range(1, TENANTS):
        row = jnp.where(tenant == k, table[k : k + 1], row)
    return row


def hbm_specs(n):
    return [pl.BlockSpec(memory_space=pltpu.HBM)] * n


def vmem_specs(n):
    return [pl.BlockSpec(memory_space=pltpu.VMEM)] * n


def half_scratch():
    return [
        pltpu.VMEM((8, DEPTH, PANEL), bf16),
        pltpu.VMEM((8, DEPTH, BACK), bf16),
        pltpu.VMEM((8, SPAN, WIDTH), bf16),
    ]


def run_held(meta, tok, front, back):
    rows = RING * LEN
    return pl.pallas_call(
        project_held,
        in_specs=[pl.BlockSpec(memory_space=pltpu.SMEM)] + hbm_specs(12),
        out_specs=vmem_specs(2),
        out_shape=[jax.ShapeDtypeStruct((rows, n), f32) for n in (PANEL, BACK)],
        scratch_shapes=half_scratch()
        + [pltpu.SemaphoreType.DMA((2,)), pltpu.SemaphoreType.DMA((8,))],
        compiler_params=pltpu.CompilerParams(vmem_limit_bytes=48 << 20),
        cost_estimate=pl.CostEstimate(
            flops=rows * WIDTH * (PANEL + BACK), bytes_accessed=20 << 20, transcendentals=0
        ),
        name="project_held",
    )(meta, *tok, *front, *back)


def run_came(meta, tok, front, front_came, back_came, up, mag, bias, rate, bases):
    rows = RING * LEN
    heads = jax.ShapeDtypeStruct((RING, LEN, GROUP_HEADS), f32)
    return pl.pallas_call(
        project_came,
        grid_spec=pltpu.PrefetchScalarGridSpec(
            num_scalar_prefetch=1,
            grid=(1,),
            in_specs=hbm_specs(14)
            + [
                pl.BlockSpec((TENANTS * RANK, GROUP_COLS), lambda i, m: (0, m[1])),
                pl.BlockSpec((TENANTS, GROUP_COLS), lambda i, m: (0, m[1])),
            ]
            + vmem_specs(4),
            out_specs=hbm_specs(4) + vmem_specs(3),
            scratch_shapes=half_scratch()
            + [
                pltpu.VMEM((rows, PANEL), f32),
                pltpu.VMEM((rows, BACK), f32),
                pltpu.VMEM((RING, LEN, GROUP_COLS), bf16),
                pltpu.VMEM((16, NORM_ROWS, PANEL), bf16),
                pltpu.SemaphoreType.DMA((2,)),
                pltpu.SemaphoreType.DMA((8,)),
                pltpu.SemaphoreType.DMA((RING,)),
                pltpu.SemaphoreType.DMA,
            ],
        ),
        out_shape=[jax.ShapeDtypeStruct((LEN, GROUP_COLS), bf16)] * RING
        + [heads, heads, jax.ShapeDtypeStruct((RING, GROUP_HEADS, LEN), f32)],
        compiler_params=pltpu.CompilerParams(vmem_limit_bytes=48 << 20),
        cost_estimate=pl.CostEstimate(
            flops=rows * WIDTH * (PANEL + BACK), bytes_accessed=20 << 20, transcendentals=0
        ),
        name="project_came",
    )(meta, *tok, *front, *front_came, *back_came, up, mag, bias, rate, *bases)


def contract_first(a, b):
    return lax.dot_general(a, b, (((0,), (0,)), ((), ())), preferred_element_type=f32)


def contract_last(a, b):
    return lax.dot_general(a, b, (((1,), (1,)), ((), ())), preferred_element_type=f32)


def scan_kernel(aliased, meta, *refs):
    projected, taps, offset, gain, skip, step_ref, cumul_ref, cumul_t_ref, cot_own, cot_other = refs[:10]
    refs = refs[10 + aliased :]
    mixed_ref, grad_ref, send_ref = refs[:3]
    padded, conv, raws, grads, incoming, outgoing, mixed_all, x_all = refs[3:]
    c, length = meta[0], meta[2]
    pairs = GROUP_HEADS // 2
    padded[0:8, :] = jnp.zeros((8, GROUP_COLS), f32)
    padded[8:, :] = projected[...].astype(f32)
    summed = offset[...] + taps[0:1, :] * padded[5 : 5 + LEN, :]
    for i in range(1, CONV):
        summed = summed + taps[i : i + 1, :] * padded[5 + i : 5 + i + LEN, :]
    conv[...] = (summed / (1.0 + jnp.exp(-summed))).astype(bf16)
    causal = lax.broadcasted_iota(jnp.int32, (SPAN, SPAN), 0) >= lax.broadcasted_iota(
        jnp.int32, (SPAN, SPAN), 1
    )
    anti = lax.broadcasted_iota(jnp.int32, (SPAN, SPAN), 0) <= lax.broadcasted_iota(
        jnp.int32, (SPAN, SPAN), 1
    )
    low_lane = lax.broadcasted_iota(jnp.int32, (SPAN, SPAN), 1) < HEAD_DIM

    def spread(ref, rows, head):
        return jnp.broadcast_to(ref[0, rows, head : head + 1], (SPAN, SPAN))

    def stacked(values):
        zero = jnp.zeros_like(values)
        return jnp.concatenate(
            [jnp.where(low_lane, values, zero), jnp.where(low_lane, zero, values)], axis=0
        )

    for block in range(LEN // SPAN):
        rows = slice(block * SPAN, (block + 1) * SPAN)
        keys = conv[rows, GROUP_CHANNELS : GROUP_CHANNELS + STATE]
        queries = conv[rows, GROUP_CHANNELS + STATE :]
        scores = jnp.where(causal, contract_last(queries, keys), 0.0)
        squares = jnp.zeros((SPAN, SPAN), f32)
        for q in range(pairs):
            lanes = slice(q * SPAN, (q + 1) * SPAN)
            values = conv[rows, lanes].astype(f32)
            level = [spread(cumul_ref, rows, 2 * q + i) for i in range(2)]
            mix = [
                (
                    jnp.exp(jnp.minimum(level[i] - cumul_t_ref[0, 2 * q + i : 2 * q + i + 1, rows], 0.0))
                    * scores
                ).astype(bf16)
                for i in range(2)
            ]
            step = jnp.where(low_lane, spread(step_ref, rows, 2 * q), spread(step_ref, rows, 2 * q + 1))
            inflow = (step * values).astype(bf16)
            raw = jnp.dot(
                jnp.concatenate(mix, axis=1), stacked(inflow), preferred_element_type=f32
            )
            both = jnp.where(low_lane, level[0], level[1])
            if block == 0:
                tail = jnp.exp(both[SPAN - 1 :, :] - both)
                scaled = (inflow.astype(f32) * tail).astype(bf16)
                incoming[:, lanes] = contract_first(keys, scaled).astype(bf16)
            else:
                raw = raw + jnp.dot(
                    queries, incoming[:, lanes], preferred_element_type=f32
                ) * jnp.exp(both)
            raw = raw + skip[:, lanes] * values
            raws[rows, lanes] = raw
            squares = squares + raw * raw
        mean_sq = jnp.sum(squares, axis=1, keepdims=True) / GROUP_CHANNELS
        inverse = lax.rsqrt(mean_sq + eps_norm)
        at = block * SPAN + lax.broadcasted_iota(jnp.int32, (SPAN, 1), 0)
        live = jnp.where(at < length, 1.0, 0.0)
        upstream = jnp.where(c == block, cot_own[...], cot_other[...]).astype(f32) * live
        raw = raws[rows, :]
        scaled_up = upstream * gain[...]
        mixed_all[rows, :] = ((gain[...] * raw) * (inverse * live)).astype(bf16)
        along = jnp.sum(scaled_up * raw, axis=1, keepdims=True) / GROUP_CHANNELS
        grads[rows, :] = scaled_up * inverse - raw * (along * inverse * inverse * inverse)

    for block in reversed(range(LEN // SPAN)):
        rows = slice(block * SPAN, (block + 1) * SPAN)
        keys = conv[rows, GROUP_CHANNELS : GROUP_CHANNELS + STATE]
        queries = conv[rows, GROUP_CHANNELS + STATE :]
        scores = jnp.where(anti, contract_last(keys, queries), 0.0)
        for q in range(pairs):
            lanes = slice(q * SPAN, (q + 1) * SPAN)
            level = [spread(cumul_ref, rows, 2 * q + i) for i in range(2)]
            mix = [
                (
                    jnp.exp(jnp.minimum(cumul_t_ref[0, 2 * q + i : 2 * q + i + 1, rows] - level[i], 0.0))
                    * scores
                ).astype(bf16)
                for i in range(2)
            ]
            step = jnp.where(low_lane, spread(step_ref, rows, 2 * q), spread(step_ref, rows, 2 * q + 1))
            grad = grads[rows, lanes]
            back = jnp.dot(
                jnp.concatenate(mix, axis=1), stacked(grad.astype(bf16)), preferred_element_type=f32
            )
            both = jnp.where(low_lane, level[0], level[1])
            if block == 1:
                weighted = (grad * jnp.exp(both)).astype(bf16)
                outgoing[:, lanes] = contract_first(queries, weighted).astype(bf16)
            else:
                tail = jnp.exp(both[SPAN - 1 :, :] - both)
                back = back + jnp.dot(keys, outgoing[:, lanes], preferred_element_type=f32) * tail
            x_all[rows, lanes] = (skip[:, lanes] * grad + step * back).astype(bf16)

    mine = pl.ds(pl.multiple_of(c * SPAN, SPAN), SPAN)
    others = pl.ds(pl.multiple_of((1 - c) * SPAN, SPAN), SPAN)
    mixed_ref[...] = mixed_all[mine, :]
    grad_ref[...] = x_all[mine, :]
    send_ref[0] = mixed_all[others, :]
    send_ref[1] = x_all[others, :]


def run_scan(d, meta, projected, shared, cot, cot_other, totals):
    taps, offset, gain, skip, step, cumul, cumul_t = shared
    out_full = jax.ShapeDtypeStruct((SPAN, GROUPS * GROUP_CHANNELS), bf16)

    def local(m):
        return (m[1] + d) % RING

    def whole(m):
        return m[0] * RING + local(m)

    aliased = 0 if totals is None else 2
    extra = () if totals is None else tuple(totals)

    def kernel(*refs):
        scan_kernel(aliased, *refs)

    return pl.pallas_call(
        kernel,
        grid_spec=pltpu.PrefetchScalarGridSpec(
            num_scalar_prefetch=1,
            grid=(1,),
            in_specs=[
                pl.BlockSpec((LEN, GROUP_COLS), lambda i, m: (0, 0)),
                pl.BlockSpec((CONV, GROUP_COLS), lambda i, m: (0, whole(m))),
                pl.BlockSpec((1, GROUP_COLS), lambda i, m: (0, whole(m))),
                pl.BlockSpec((1, GROUP_CHANNELS), lambda i, m: (0, whole(m))),
                pl.BlockSpec((1, GROUP_CHANNELS), lambda i, m: (0, whole(m))),
                pl.BlockSpec((1, LEN, GROUP_HEADS), lambda i, m: (local(m), 0, 0)),
                pl.BlockSpec((1, LEN, GROUP_HEADS), lambda i, m: (local(m), 0, 0)),
                pl.BlockSpec((1, GROUP_HEADS, LEN), lambda i, m: (local(m), 0, 0)),
                pl.BlockSpec((SPAN, GROUP_CHANNELS), lambda i, m: (0, whole(m))),
                pl.BlockSpec((SPAN, GROUP_CHANNELS), lambda i, m: (0, local(m))),
            ]
            + hbm_specs(aliased),
            out_specs=[
                pl.BlockSpec((SPAN, GROUP_CHANNELS), lambda i, m: (0, whole(m))),
                pl.BlockSpec((SPAN, GROUP_CHANNELS), lambda i, m: (0, whole(m))),
                pl.BlockSpec((2, SPAN, GROUP_CHANNELS), lambda i, m: (0, 0, 0)),
            ],
            scratch_shapes=[
                pltpu.VMEM((LEN + 8, GROUP_COLS), f32),
                pltpu.VMEM((LEN, GROUP_COLS), bf16),
                pltpu.VMEM((LEN, GROUP_CHANNELS), f32),
                pltpu.VMEM((LEN, GROUP_CHANNELS), f32),
                pltpu.VMEM((STATE, GROUP_CHANNELS), bf16),
                pltpu.VMEM((STATE, GROUP_CHANNELS), bf16),
                pltpu.VMEM((LEN, GROUP_CHANNELS), bf16),
                pltpu.VMEM((LEN, GROUP_CHANNELS), bf16),
            ],
        ),
        out_shape=[out_full, out_full, jax.ShapeDtypeStruct((2, SPAN, GROUP_CHANNELS), bf16)],
        input_output_aliases={} if totals is None else {11: 0, 12: 1},
        compiler_params=pltpu.CompilerParams(vmem_limit_bytes=60 << 20),
        cost_estimate=pl.CostEstimate(flops=6 << 30, bytes_accessed=4 << 20, transcendentals=0),
        name="scan_group",
    )(meta, projected, taps, offset, gain, skip, step, cumul, cumul_t, cot, cot_other, *extra)


def split_sum(values):
    high = lax.reduce_precision(values, 8, 7)
    return high.astype(bf16), (values - high).astype(bf16)


def norm_rows(sums):
    high, low = split_sum(sums)
    parts = [part[..., i * PANEL : (i + 1) * PANEL] for i in range(2) for part in (high, low)]
    return jnp.concatenate(parts, axis=-2)


def per_device(
    tokens,
    weight,
    adapter_down_weight,
    adapter_up_weight,
    magnitude,
    step_size_weight,
    step_size_bias,
    decay_rate_log,
    head_skip_gain,
    convolution_weight,
    convolution_bias,
    grouped_norm_gain,
    tenant,
    lengths,
    cotangent,
):
    c, x, y, z = (lax.axis_index(name) for name in ("seq", "x", "y", "z"))
    own_tokens = tokens[0]
    upstream = cotangent[0]
    by_chip = jnp.swapaxes(weight.reshape(ROWS, RING, GROUP_COLS), 0, 1)

    def round_x(block):
        return [
            block[0],
            shift(block[3], "x", -1),
            shift(block[2], "x", 2),
            shift(block[1], "x", 1),
        ]

    tie = lax.optimization_barrier

    def grown(part, axis, near):
        return jnp.concatenate([part, swap(part, axis, near)], axis=0)

    adapted = weight.astype(f32)[None] + jnp.einsum(
        "gbc,bco->bgo", adapter_down_weight, adapter_up_weight, preferred_element_type=f32
    )
    sums = jnp.sum(adapted * adapted, axis=1).reshape(TENANTS, RING, GROUP_COLS)
    marks = norm_rows(jnp.swapaxes(sums, 0, 1))
    heads_here = HEADS // 2
    extras = jnp.concatenate(
        [
            lax.dynamic_slice_in_dim(step_size_weight, c * heads_here, heads_here, 1),
            adapter_down_weight.reshape(ROWS, TENANTS * RANK),
        ],
        axis=1,
    )
    tenant_mark = jnp.broadcast_to(tenant[0].astype(bf16), (RING, NORM_ROWS, EXTRA))
    back_mark = jnp.zeros((RING, NORM_ROWS, BACK), bf16)
    blocks = jnp.concatenate(
        [
            jnp.concatenate(
                [
                    by_chip[:, :, :FRONT],
                    jnp.broadcast_to(extras, (RING, ROWS, EXTRA)),
                    by_chip[:, :, FRONT:],
                ],
                axis=2,
            ),
            jnp.concatenate([marks, tenant_mark, back_mark[:, :, EXTRA:]], axis=2),
        ],
        axis=1,
    )

    blocks = round_x([pick(blocks, (x + d) % RING) for d in range(RING)])
    tenants = [tenant[0]] + [blocks[i][ROWS, PANEL].astype(jnp.int32) for i in (3, 1, 2)]
    rows = place_order(*[part[:ROWS] for part in blocks], x).reshape(DEPTH, GROUP_COLS + EXTRA)
    sums = sum(part[ROWS:, :PANEL].astype(f32) for part in blocks)
    sums = jnp.concatenate([sums[0:4] + sums[4:8], sums[8:12] + sums[12:16]], axis=1)
    front = jnp.concatenate([rows[:, :PANEL], norm_rows(sums)], axis=0)[None]
    back = rows[None, :, PANEL:]

    def grown(part, axis, near):
        return jnp.concatenate([part, swap(part, axis, near)], axis=0)

    per_core = GROUPS // 2 * GROUP_CHANNELS
    cot_other = lax.dynamic_slice_in_dim(upstream, (1 - c) * per_core, per_core, 1)
    front, back, own_tokens, cot_other = tie((front, back, own_tokens, cot_other))
    crossed = [cross(own_tokens)]
    front, back = grown(front, "y", True), grown(back, "z", True)
    front, back, own_tokens, crossed, cot_other = tie((front, back, own_tokens, crossed, cot_other))
    one, cot_other = turn(own_tokens, "x", 1), cross(cot_other)
    front, back = grown(front, "z", True), grown(back, "y", True)
    front, back, one, own_tokens, cot_other = tie((front, back, one, own_tokens, cot_other))
    two, three = turn(own_tokens, "x", -1), turn(one, "x", 1)
    crossed = crossed + [cross(one)]
    front, back = [front, swap(front, "y", False)], [back, swap(back, "z", False)]
    front, back, two, crossed = tie((front, back, two, crossed))
    front_came = [swap(part, "z", False) for part in front]
    back_came = [swap(part, "y", False) for part in back]
    crossed = crossed + [cross(two), cross(three)]

    up = adapter_up_weight.reshape(TENANTS * RANK, RING * GROUP_COLS)
    place = jnp.stack([c, x, y, z]).astype(jnp.int32)
    meta = jnp.concatenate([place, jnp.stack(tenants)])
    tok = [own_tokens, one, two, three] + crossed
    bases = run_held(place, tok, front, back)
    *projected, step_size, cumul, cumul_t = run_came(
        meta,
        tok,
        front,
        front_came,
        back_came,
        up,
        magnitude,
        step_size_bias[None],
        decay_rate_log[None],
        bases,
    )
    shared = (
        convolution_weight,
        convolution_bias[None],
        grouped_norm_gain[None],
        jnp.repeat(head_skip_gain, HEAD_DIM)[None],
        step_size,
        cumul,
        cumul_t,
    )

    own, to_left, to_right, to_opposite = projected
    from_right, from_left = shift(to_left, "x", -1), shift(to_right, "x", 1)
    to_opposite = tie((to_opposite, from_left, from_right))[0]
    projected = [own, from_right, from_left, shift(to_opposite, "x", 2)]
    totals = None
    sends = []
    scan_meta = jnp.stack([c, x, lengths[0]]).astype(jnp.int32)
    for i, d in ((0, 0), (1, 1), (2, 3), (3, 2)):
        group = (x + d) % RING
        *totals, send = run_scan(
            d, scan_meta, projected[i], shared, upstream, cot_other, totals
        )
        sends.append((group, cross(send)))
    mixed, x_grad = totals
    for group, got in sends:
        at = (RING * (1 - c) + group) * GROUP_CHANNELS
        mixed = lax.dynamic_update_slice_in_dim(mixed, got[0], at, 1)
        x_grad = lax.dynamic_update_slice_in_dim(x_grad, got[1], at, 1)
    return (mixed[None], x_grad[None])


def solution(mesh):
    chips = Mesh(mesh.devices.reshape(2, RING, RING, RING), ("seq", "z", "y", "x"))
    fsdp = ("z", "y", "x")
    return jax.shard_map(
        per_device,
        mesh=chips,
        in_specs=(
            P(fsdp, "seq", None),
            P(fsdp, "seq"),
            P(fsdp, None, None),
            P(None, None, "seq"),
            P(None, "seq"),
            P(fsdp, None),
            P(),
            P(),
            P(),
            P(),
            P(),
            P(),
            P(fsdp),
            P(fsdp),
            P(fsdp, "seq", None),
        ),
        out_specs=(P(fsdp, "seq", None), P(fsdp, "seq", None)),
        check_vma=False,
    )
```

```python
import jax
import jax.numpy as jnp
from jax import lax
from jax.experimental import pallas as pl
from jax.experimental.pallas import tpu as pltpu
from jax.sharding import Mesh, PartitionSpec as P

HEADS = 128
HEAD_DIM = 64
GROUPS = 8
STATE = 128
CONV = 4
SPAN = 128
RING = 4
ROWS = 64
WIDTH = 4096
LEN = 256
TENANTS = 4
RANK = 16
FRONT = 512
GROUP_COLS = 1280
BACK = GROUP_COLS - FRONT
GROUP_CHANNELS = 1024
GROUP_HEADS = 16
EXTRA = 128
PANEL = FRONT + EXTRA
NORM_ROWS = 16
DEPTH = 256

eps_norm = 1e-05
eps_column = 1e-06

f32 = jnp.float32
bf16 = jnp.bfloat16


def shift(v, axis, by):
    return lax.ppermute(v, axis, [(i, (i + by) % RING) for i in range(RING)])


def turn(v, axis, by):
    steps = (by, -by)
    return lax.ppermute(
        v,
        ("seq", axis),
        [(k * RING + i, k * RING + (i + steps[k]) % RING) for k in range(2) for i in range(RING)],
    )


def swap(v, axis, near):
    masks = (1, 3) if near else (3, 1)
    return lax.ppermute(
        v,
        ("seq", axis),
        [(k * RING + i, k * RING + (i ^ masks[k])) for k in range(2) for i in range(RING)],
    )


def cross(v):
    return lax.ppermute(v, "seq", [(0, 1), (1, 0)])


def pick(v, index):
    return lax.dynamic_index_in_dim(v, index, 0, keepdims=False)


def place_order(own, right, opposite, left, x):
    twice = jnp.stack([own, right, opposite, left, own, right, opposite, left])
    return lax.dynamic_slice_in_dim(twice, (RING - x) % RING, RING, 0)


def wait_all(ref, sem):
    pltpu.make_async_copy(ref, ref, sem).wait()


def bits(own, at, c):
    gap = own ^ at
    far = gap >> 1
    near = (gap ^ far) & 1
    return jnp.where(c == 0, near, far), jnp.where(c == 0, far, near)


def half_ranges(meta, order, came):
    c, y, z = meta[0], meta[2], meta[3]
    near, far = 1 + 2 * c, 3 - 2 * c
    split = z if order == "yz" else y
    places = [split ^ (came * far) ^ (i * near) for i in range(2)]
    if order == "yz":
        width = RING * DEPTH
        starts = [place * width for place in places]
    else:
        width = DEPTH
        starts = [(at * RING + place) * width for at in range(RING) for place in places]
    return [pl.multiple_of(start, DEPTH) for start in starts], width


def half_copies(meta, order, panel_refs, panel, sem):
    other = meta[2] if order == "yz" else meta[3]
    for at in range(RING):
        first, second = bits(other, at, meta[0])
        for i in range(2):
            slot = i * RING + at if order == "yz" else at * 2 + i
            for half in range(2):

                @pl.when(second == half)
                def _(i=i, half=half, first=first, slot=slot):
                    pltpu.make_async_copy(
                        panel_refs[half].at[first + 2 * i, pl.ds(0, DEPTH), :], panel.at[slot], sem
                    ).start()


def piece_copies(tok_refs, pieces, sem):
    for i, ref in enumerate(tok_refs):
        pltpu.make_async_copy(ref, pieces.at[i], sem.at[i]).start()


def half_products(meta, order, came, pieces, piece_sem, panel, emit):
    c = meta[0]
    starts, width = half_ranges(meta, order, came)
    for source, place in ((0, c), (1, 1 - c)):
        sequences = (0, 1 + place, 2 - place, 3)
        for i, sequence in enumerate(sequences):
            at = 4 * source + i
            if piece_sem is not None:
                wait_all(pieces.at[at], piece_sem.at[at])
            rows = pl.ds(pl.multiple_of(sequence * LEN + place * SPAN, SPAN), SPAN)
            piece = jnp.concatenate([pieces[at, :, pl.ds(start, width)] for start in starts], axis=1)
            whole = panel[...].reshape(WIDTH // 2, panel.shape[-1])
            emit(rows, jnp.dot(piece, whole, preferred_element_type=f32))


def project_held(meta, *refs):
    tok_refs, front_ref, back_ref = refs[:8], refs[8:10], refs[10:12]
    front_out, back_out, front_panel, back_panel, pieces, sem, piece_sem = refs[12:]
    parts = (("yz", front_ref, front_panel, front_out), ("zy", back_ref, back_panel, back_out))
    for i, (order, ref, panel, _) in enumerate(parts):
        half_copies(meta, order, ref, panel, sem.at[i])
        if i == 0:
            piece_copies(tok_refs, pieces, piece_sem)
    for i, (order, _, panel, out) in enumerate(parts):
        wait_all(panel, sem.at[i])

        def emit(rows, product, out=out):
            out[rows, :] = product

        half_products(meta, order, 0, pieces, piece_sem if i == 0 else None, panel, emit)


def project_came(meta, *refs):
    tok_refs, front_held, front_ref, back_ref = refs[:8], refs[8:10], refs[10:12], refs[12:14]
    up_ref, mag_ref, bias_ref, rate_ref, front_base, back_base = refs[14:20]
    outs = refs[20:24]
    step_out, cumul_out, cumul_t_out = refs[24:27]
    front_panel, back_panel, pieces, front_acc, back_acc, ready, norms = refs[27:34]
    sem, piece_sem, ready_sem, norm_sem = refs[34:]
    c = meta[0]
    for i, ref in enumerate((*front_held, *front_ref)):
        pltpu.make_async_copy(
            ref.at[:, pl.ds(DEPTH, NORM_ROWS), :], norms.at[pl.ds(4 * i, 4)], norm_sem
        ).start()
    parts = (
        ("yz", front_ref, front_panel, front_base, front_acc),
        ("zy", back_ref, back_panel, back_base, back_acc),
    )
    for i, (order, ref, panel, _, _) in enumerate(parts):
        half_copies(meta, order, ref, panel, sem.at[i])
        if i == 0:
            piece_copies(tok_refs, pieces, piece_sem)
    wait_all(norms, norm_sem)
    total = jnp.sum(norms[...].astype(f32), axis=0)
    squares = [total[8 * i : 8 * i + 4] + total[8 * i + 4 : 8 * i + 8] for i in range(2)]
    squares = jnp.concatenate(squares, axis=1)
    scale = mag_ref[...] / jnp.sqrt(squares + eps_column)
    up = padded_up(up_ref)
    for i, (order, _, panel, base, acc) in enumerate(parts):
        wait_all(panel, sem.at[i])

        def emit(rows, product, base=base, acc=acc):
            acc[rows, :] = base[rows, :] + product

        half_products(meta, order, 1, pieces, piece_sem if i == 0 else None, panel, emit)
    lane_tenant = lax.broadcasted_iota(jnp.int32, (LEN, EXTRA), 1) // RANK - RING
    for s in (1, 2, 3, 0):
        tenant = meta[4 + s]
        rows = pl.ds(s * LEN, LEN)
        low = jnp.where(lane_tenant == tenant, front_acc[rows, FRONT:], 0.0).astype(bf16)
        for acc, cols in ((front_acc, slice(0, FRONT)), (back_acc, slice(FRONT, GROUP_COLS))):
            result = acc[rows, : cols.stop - cols.start] + jnp.dot(
                low, up[:, cols], preferred_element_type=f32
            )
            ready[s, :, cols] = (result * tenant_row(scale[:, cols], tenant)).astype(bf16)
        pltpu.make_async_copy(ready.at[s], outs[s], ready_sem.at[s]).start()
    heads_here = HEADS // 2
    bias = jnp.where(c == 0, bias_ref[:, :heads_here], bias_ref[:, heads_here:])
    rate = jnp.where(c == 0, rate_ref[:, :heads_here], rate_ref[:, heads_here:])
    raw = front_acc[0:LEN, FRONT : FRONT + heads_here] + bias
    step = jnp.maximum(raw, 0.0) + jnp.log1p(jnp.exp(-jnp.abs(raw)))
    logdecay = -step * jnp.exp(rate)
    ones = jnp.where(
        lax.broadcasted_iota(jnp.int32, (SPAN, SPAN), 0)
        >= lax.broadcasted_iota(jnp.int32, (SPAN, SPAN), 1),
        1.0,
        0.0,
    )
    for block in range(LEN // SPAN):
        rows = slice(block * SPAN, (block + 1) * SPAN)
        cumul = jnp.dot(
            ones, logdecay[rows], precision=lax.Precision.HIGHEST, preferred_element_type=f32
        )
        cumul_t = cumul.T
        for g in range(RING):
            heads = slice(g * GROUP_HEADS, (g + 1) * GROUP_HEADS)
            step_out[g, rows, :] = step[rows, heads]
            cumul_out[g, rows, :] = cumul[:, heads]
            cumul_t_out[g, :, rows] = cumul_t[heads, :]
    for s in range(RING):
        pltpu.make_async_copy(ready.at[s], outs[s], ready_sem.at[s]).wait()


def padded_up(up_ref):
    return jnp.concatenate([jnp.zeros((EXTRA - TENANTS * RANK, GROUP_COLS), bf16), up_ref[...]], axis=0)


def tenant_row(table, tenant):
    row = table[0:1]
    for k in range(1, TENANTS):
        row = jnp.where(tenant == k, table[k : k + 1], row)
    return row


def hbm_specs(n):
    return [pl.BlockSpec(memory_space=pltpu.HBM)] * n


def vmem_specs(n):
    return [pl.BlockSpec(memory_space=pltpu.VMEM)] * n


def half_scratch():
    return [
        pltpu.VMEM((8, DEPTH, PANEL), bf16),
        pltpu.VMEM((8, DEPTH, BACK), bf16),
        pltpu.VMEM((8, SPAN, WIDTH), bf16),
    ]


def run_held(meta, tok, front, back):
    rows = RING * LEN
    return pl.pallas_call(
        project_held,
        in_specs=[pl.BlockSpec(memory_space=pltpu.SMEM)] + hbm_specs(12),
        out_specs=vmem_specs(2),
        out_shape=[jax.ShapeDtypeStruct((rows, n), f32) for n in (PANEL, BACK)],
        scratch_shapes=half_scratch()
        + [pltpu.SemaphoreType.DMA((2,)), pltpu.SemaphoreType.DMA((8,))],
        compiler_params=pltpu.CompilerParams(vmem_limit_bytes=48 << 20),
        cost_estimate=pl.CostEstimate(
            flops=rows * WIDTH * (PANEL + BACK), bytes_accessed=20 << 20, transcendentals=0
        ),
        name="project_held",
    )(meta, *tok, *front, *back)


def run_came(meta, tok, front, front_came, back_came, up, mag, bias, rate, bases):
    rows = RING * LEN
    heads = jax.ShapeDtypeStruct((RING, LEN, GROUP_HEADS), f32)
    return pl.pallas_call(
        project_came,
        grid_spec=pltpu.PrefetchScalarGridSpec(
            num_scalar_prefetch=1,
            grid=(1,),
            in_specs=hbm_specs(14)
            + [
                pl.BlockSpec((TENANTS * RANK, GROUP_COLS), lambda i, m: (0, m[1])),
                pl.BlockSpec((TENANTS, GROUP_COLS), lambda i, m: (0, m[1])),
            ]
            + vmem_specs(4),
            out_specs=hbm_specs(4) + vmem_specs(3),
            scratch_shapes=half_scratch()
            + [
                pltpu.VMEM((rows, PANEL), f32),
                pltpu.VMEM((rows, BACK), f32),
                pltpu.VMEM((RING, LEN, GROUP_COLS), bf16),
                pltpu.VMEM((16, NORM_ROWS, PANEL), bf16),
                pltpu.SemaphoreType.DMA((2,)),
                pltpu.SemaphoreType.DMA((8,)),
                pltpu.SemaphoreType.DMA((RING,)),
                pltpu.SemaphoreType.DMA,
            ],
        ),
        out_shape=[jax.ShapeDtypeStruct((LEN, GROUP_COLS), bf16)] * RING
        + [heads, heads, jax.ShapeDtypeStruct((RING, GROUP_HEADS, LEN), f32)],
        compiler_params=pltpu.CompilerParams(vmem_limit_bytes=48 << 20),
        cost_estimate=pl.CostEstimate(
            flops=rows * WIDTH * (PANEL + BACK), bytes_accessed=20 << 20, transcendentals=0
        ),
        name="project_came",
    )(meta, *tok, *front, *front_came, *back_came, up, mag, bias, rate, *bases)


def contract_first(a, b):
    return lax.dot_general(a, b, (((0,), (0,)), ((), ())), preferred_element_type=f32)


def contract_last(a, b):
    return lax.dot_general(a, b, (((1,), (1,)), ((), ())), preferred_element_type=f32)


def scan_kernel(aliased, meta, *refs):
    projected, taps, offset, gain, skip, step_ref, cumul_ref, cumul_t_ref, cot_own, cot_other = refs[:10]
    refs = refs[10 + aliased :]
    mixed_ref, grad_ref, send_ref = refs[:3]
    padded, conv, raws, grads, incoming, outgoing, mixed_all, x_all, steps, boths, mixes = refs[3:]
    c, length = meta[0], meta[2]
    pairs = GROUP_HEADS // 2
    padded[0:8, :] = jnp.zeros((8, GROUP_COLS), f32)
    padded[8:, :] = projected[...].astype(f32)
    summed = offset[...] + taps[0:1, :] * padded[5 : 5 + LEN, :]
    for i in range(1, CONV):
        summed = summed + taps[i : i + 1, :] * padded[5 + i : 5 + i + LEN, :]
    conv[...] = (summed / (1.0 + jnp.exp(-summed))).astype(bf16)
    causal = lax.broadcasted_iota(jnp.int32, (SPAN, SPAN), 0) >= lax.broadcasted_iota(
        jnp.int32, (SPAN, SPAN), 1
    )
    anti = lax.broadcasted_iota(jnp.int32, (SPAN, SPAN), 0) <= lax.broadcasted_iota(
        jnp.int32, (SPAN, SPAN), 1
    )
    low_lane = lax.broadcasted_iota(jnp.int32, (SPAN, SPAN), 1) < HEAD_DIM

    def spread(ref, rows, head):
        return jnp.broadcast_to(ref[0, rows, head : head + 1], (SPAN, SPAN))

    def stacked(values):
        zero = jnp.zeros_like(values)
        return jnp.concatenate(
            [jnp.where(low_lane, values, zero), jnp.where(low_lane, zero, values)], axis=0
        )

    for block in range(LEN // SPAN):
        rows = slice(block * SPAN, (block + 1) * SPAN)
        keys = conv[rows, GROUP_CHANNELS : GROUP_CHANNELS + STATE]
        queries = conv[rows, GROUP_CHANNELS + STATE :]
        scores = jnp.where(causal, contract_last(queries, keys), 0.0)
        squares = jnp.zeros((SPAN, SPAN), f32)
        for q in range(pairs):
            lanes = slice(q * SPAN, (q + 1) * SPAN)
            values = conv[rows, lanes].astype(f32)
            level = [spread(cumul_ref, rows, 2 * q + i) for i in range(2)]
            mix = [
                (
                    jnp.exp(jnp.minimum(level[i] - cumul_t_ref[0, 2 * q + i : 2 * q + i + 1, rows], 0.0))
                    * scores
                ).astype(bf16)
                for i in range(2)
            ]
            step = jnp.where(low_lane, spread(step_ref, rows, 2 * q), spread(step_ref, rows, 2 * q + 1))
            steps[rows, lanes] = step
            inflow = (step * values).astype(bf16)
            mixes[block, q, :SPAN] = mix[0]
            mixes[block, q, SPAN:] = mix[1]
            raw = jnp.dot(
                jnp.concatenate(mix, axis=1), stacked(inflow), preferred_element_type=f32
            )
            both = jnp.where(low_lane, level[0], level[1])
            if block == 0:
                tail = jnp.exp(both[SPAN - 1 :, :] - both)
                boths[rows, lanes] = tail
                scaled = (inflow.astype(f32) * tail).astype(bf16)
                incoming[:, lanes] = contract_first(keys, scaled).astype(bf16)
            else:
                growth = jnp.exp(both)
                boths[rows, lanes] = growth
                raw = raw + jnp.dot(
                    queries, incoming[:, lanes], preferred_element_type=f32
                ) * growth
            raw = raw + skip[:, lanes] * values
            raws[rows, lanes] = raw
            squares = squares + raw * raw
        mean_sq = jnp.sum(squares, axis=1, keepdims=True) / GROUP_CHANNELS
        inverse = lax.rsqrt(mean_sq + eps_norm)
        at = block * SPAN + lax.broadcasted_iota(jnp.int32, (SPAN, 1), 0)
        live = jnp.where(at < length, 1.0, 0.0)
        upstream = jnp.where(c == block, cot_own[...], cot_other[...]).astype(f32) * live
        raw = raws[rows, :]
        scaled_up = upstream * gain[...]
        mixed_all[rows, :] = ((gain[...] * raw) * (inverse * live)).astype(bf16)
        along = jnp.sum(scaled_up * raw, axis=1, keepdims=True) / GROUP_CHANNELS
        grads[rows, :] = scaled_up * inverse - raw * (along * inverse * inverse * inverse)

    for block in reversed(range(LEN // SPAN)):
        rows = slice(block * SPAN, (block + 1) * SPAN)
        keys = conv[rows, GROUP_CHANNELS : GROUP_CHANNELS + STATE]
        queries = conv[rows, GROUP_CHANNELS + STATE :]
        for q in range(pairs):
            lanes = slice(q * SPAN, (q + 1) * SPAN)
            step = steps[rows, lanes]
            grad = grads[rows, lanes]
            back = contract_first(mixes[block, q], stacked(grad.astype(bf16)))
            if block == 1:
                weighted = (grad * boths[rows, lanes]).astype(bf16)
                outgoing[:, lanes] = contract_first(queries, weighted).astype(bf16)
            else:
                back = back + jnp.dot(
                    keys, outgoing[:, lanes], preferred_element_type=f32
                ) * boths[rows, lanes]
            x_all[rows, lanes] = (skip[:, lanes] * grad + step * back).astype(bf16)

    mine = pl.ds(pl.multiple_of(c * SPAN, SPAN), SPAN)
    others = pl.ds(pl.multiple_of((1 - c) * SPAN, SPAN), SPAN)
    mixed_ref[...] = mixed_all[mine, :]
    grad_ref[...] = x_all[mine, :]
    send_ref[0] = mixed_all[others, :]
    send_ref[1] = x_all[others, :]


def run_scan(d, meta, projected, shared, cot, cot_other, totals):
    taps, offset, gain, skip, step, cumul, cumul_t = shared
    out_full = jax.ShapeDtypeStruct((SPAN, GROUPS * GROUP_CHANNELS), bf16)

    def local(m):
        return (m[1] + d) % RING

    def whole(m):
        return m[0] * RING + local(m)

    aliased = 0 if totals is None else 2
    extra = () if totals is None else tuple(totals)

    def kernel(*refs):
        scan_kernel(aliased, *refs)

    return pl.pallas_call(
        kernel,
        grid_spec=pltpu.PrefetchScalarGridSpec(
            num_scalar_prefetch=1,
            grid=(1,),
            in_specs=[
                pl.BlockSpec((LEN, GROUP_COLS), lambda i, m: (0, 0)),
                pl.BlockSpec((CONV, GROUP_COLS), lambda i, m: (0, whole(m))),
                pl.BlockSpec((1, GROUP_COLS), lambda i, m: (0, whole(m))),
                pl.BlockSpec((1, GROUP_CHANNELS), lambda i, m: (0, whole(m))),
                pl.BlockSpec((1, GROUP_CHANNELS), lambda i, m: (0, whole(m))),
                pl.BlockSpec((1, LEN, GROUP_HEADS), lambda i, m: (local(m), 0, 0)),
                pl.BlockSpec((1, LEN, GROUP_HEADS), lambda i, m: (local(m), 0, 0)),
                pl.BlockSpec((1, GROUP_HEADS, LEN), lambda i, m: (local(m), 0, 0)),
                pl.BlockSpec((SPAN, GROUP_CHANNELS), lambda i, m: (0, whole(m))),
                pl.BlockSpec((SPAN, GROUP_CHANNELS), lambda i, m: (0, local(m))),
            ]
            + hbm_specs(aliased),
            out_specs=[
                pl.BlockSpec((SPAN, GROUP_CHANNELS), lambda i, m: (0, whole(m))),
                pl.BlockSpec((SPAN, GROUP_CHANNELS), lambda i, m: (0, whole(m))),
                pl.BlockSpec((2, SPAN, GROUP_CHANNELS), lambda i, m: (0, 0, 0)),
            ],
            scratch_shapes=[
                pltpu.VMEM((LEN + 8, GROUP_COLS), f32),
                pltpu.VMEM((LEN, GROUP_COLS), bf16),
                pltpu.VMEM((LEN, GROUP_CHANNELS), f32),
                pltpu.VMEM((LEN, GROUP_CHANNELS), f32),
                pltpu.VMEM((STATE, GROUP_CHANNELS), bf16),
                pltpu.VMEM((STATE, GROUP_CHANNELS), bf16),
                pltpu.VMEM((LEN, GROUP_CHANNELS), bf16),
                pltpu.VMEM((LEN, GROUP_CHANNELS), bf16),
                pltpu.VMEM((LEN, GROUP_CHANNELS), f32),
                pltpu.VMEM((LEN, GROUP_CHANNELS), f32),
                pltpu.VMEM((2, GROUP_HEADS // 2, 2 * SPAN, SPAN), bf16),
            ],
        ),
        out_shape=[out_full, out_full, jax.ShapeDtypeStruct((2, SPAN, GROUP_CHANNELS), bf16)],
        input_output_aliases={} if totals is None else {11: 0, 12: 1},
        compiler_params=pltpu.CompilerParams(vmem_limit_bytes=60 << 20),
        cost_estimate=pl.CostEstimate(flops=6 << 30, bytes_accessed=4 << 20, transcendentals=0),
        name="scan_group",
    )(meta, projected, taps, offset, gain, skip, step, cumul, cumul_t, cot, cot_other, *extra)


def split_sum(values):
    high = lax.reduce_precision(values, 8, 7)
    return high.astype(bf16), (values - high).astype(bf16)


def norm_rows(sums):
    high, low = split_sum(sums)
    parts = [part[..., i * PANEL : (i + 1) * PANEL] for i in range(2) for part in (high, low)]
    return jnp.concatenate(parts, axis=-2)


def per_device(
    tokens,
    weight,
    adapter_down_weight,
    adapter_up_weight,
    magnitude,
    step_size_weight,
    step_size_bias,
    decay_rate_log,
    head_skip_gain,
    convolution_weight,
    convolution_bias,
    grouped_norm_gain,
    tenant,
    lengths,
    cotangent,
):
    c, x, y, z = (lax.axis_index(name) for name in ("seq", "x", "y", "z"))
    own_tokens = tokens[0]
    upstream = cotangent[0]
    by_chip = jnp.swapaxes(weight.reshape(ROWS, RING, GROUP_COLS), 0, 1)

    def round_x(block):
        return [
            block[0],
            shift(block[3], "x", -1),
            shift(block[2], "x", 2),
            shift(block[1], "x", 1),
        ]

    tie = lax.optimization_barrier

    def grown(part, axis, near):
        return jnp.concatenate([part, swap(part, axis, near)], axis=0)

    adapted = weight.astype(f32)[None] + jnp.einsum(
        "gbc,bco->bgo", adapter_down_weight, adapter_up_weight, preferred_element_type=f32
    )
    sums = jnp.sum(adapted * adapted, axis=1).reshape(TENANTS, RING, GROUP_COLS)
    marks = norm_rows(jnp.swapaxes(sums, 0, 1))
    heads_here = HEADS // 2
    extras = jnp.concatenate(
        [
            lax.dynamic_slice_in_dim(step_size_weight, c * heads_here, heads_here, 1),
            adapter_down_weight.reshape(ROWS, TENANTS * RANK),
        ],
        axis=1,
    )
    tenant_mark = jnp.broadcast_to(tenant[0].astype(bf16), (RING, NORM_ROWS, EXTRA))
    back_mark = jnp.zeros((RING, NORM_ROWS, BACK), bf16)
    blocks = jnp.concatenate(
        [
            jnp.concatenate(
                [
                    by_chip[:, :, :FRONT],
                    jnp.broadcast_to(extras, (RING, ROWS, EXTRA)),
                    by_chip[:, :, FRONT:],
                ],
                axis=2,
            ),
            jnp.concatenate([marks, tenant_mark, back_mark[:, :, EXTRA:]], axis=2),
        ],
        axis=1,
    )

    blocks = round_x([pick(blocks, (x + d) % RING) for d in range(RING)])
    tenants = [tenant[0]] + [blocks[i][ROWS, PANEL].astype(jnp.int32) for i in (3, 1, 2)]
    rows = place_order(*[part[:ROWS] for part in blocks], x).reshape(DEPTH, GROUP_COLS + EXTRA)
    sums = sum(part[ROWS:, :PANEL].astype(f32) for part in blocks)
    sums = jnp.concatenate([sums[0:4] + sums[4:8], sums[8:12] + sums[12:16]], axis=1)
    front = jnp.concatenate([rows[:, :PANEL], norm_rows(sums)], axis=0)[None]
    back = rows[None, :, PANEL:]

    def grown(part, axis, near):
        return jnp.concatenate([part, swap(part, axis, near)], axis=0)

    per_core = GROUPS // 2 * GROUP_CHANNELS
    cot_other = lax.dynamic_slice_in_dim(upstream, (1 - c) * per_core, per_core, 1)
    front, back, own_tokens, cot_other = tie((front, back, own_tokens, cot_other))
    crossed, cot_other = [cross(own_tokens)], cross(cot_other)
    front, back = grown(front, "y", True), grown(back, "z", True)
    front, back, own_tokens, crossed, cot_other = tie((front, back, own_tokens, crossed, cot_other))
    one = turn(own_tokens, "x", 1)
    front, back = grown(front, "z", True), grown(back, "y", True)
    front, back, one, own_tokens = tie((front, back, one, own_tokens))
    two, three = turn(own_tokens, "x", -1), turn(one, "x", 1)
    crossed = crossed + [cross(one)]
    front, back = [front, swap(front, "y", False)], [back, swap(back, "z", False)]
    front, back, two, crossed = tie((front, back, two, crossed))
    front_came = [swap(part, "z", False) for part in front]
    back_came = [swap(part, "y", False) for part in back]
    crossed = crossed + [cross(two), cross(three)]

    up = adapter_up_weight.reshape(TENANTS * RANK, RING * GROUP_COLS)
    place = jnp.stack([c, x, y, z]).astype(jnp.int32)
    meta = jnp.concatenate([place, jnp.stack(tenants)])
    tok = [own_tokens, one, two, three] + crossed
    bases = run_held(place, tok, front, back)
    *projected, step_size, cumul, cumul_t = run_came(
        meta,
        tok,
        front,
        front_came,
        back_came,
        up,
        magnitude,
        step_size_bias[None],
        decay_rate_log[None],
        bases,
    )
    shared = (
        convolution_weight,
        convolution_bias[None],
        grouped_norm_gain[None],
        jnp.repeat(head_skip_gain, HEAD_DIM)[None],
        step_size,
        cumul,
        cumul_t,
    )

    own, to_left, to_right, to_opposite = projected
    from_right, from_left = shift(to_left, "x", -1), shift(to_right, "x", 1)
    to_opposite = tie((to_opposite, from_left, from_right))[0]
    projected = [own, from_right, from_left, shift(to_opposite, "x", 2)]
    def written(totals, group, got):
        at = (RING * (1 - c) + group) * GROUP_CHANNELS
        return [lax.dynamic_update_slice_in_dim(v, part, at, 1) for v, part in zip(totals, got)]

    totals = None
    waiting = []
    scan_meta = jnp.stack([c, x, lengths[0]]).astype(jnp.int32)
    for i, d in ((0, 0), (1, 1), (2, 3), (3, 2)):
        if i == 3:
            for group, got in waiting[:2]:
                totals = written(totals, group, got)
            waiting = waiting[2:]
        *totals, send = run_scan(d, scan_meta, projected[i], shared, upstream, cot_other, totals)
        waiting.append(((x + d) % RING, cross(send)))
    for group, got in waiting:
        totals = written(totals, group, got)
    mixed, x_grad = totals
    return (mixed[None], x_grad[None])


def solution(mesh):
    chips = Mesh(mesh.devices.reshape(2, RING, RING, RING), ("seq", "z", "y", "x"))
    fsdp = ("z", "y", "x")
    return jax.shard_map(
        per_device,
        mesh=chips,
        in_specs=(
            P(fsdp, "seq", None),
            P(fsdp, "seq"),
            P(fsdp, None, None),
            P(None, None, "seq"),
            P(None, "seq"),
            P(fsdp, None),
            P(),
            P(),
            P(),
            P(),
            P(),
            P(),
            P(fsdp),
            P(fsdp),
            P(fsdp, "seq", None),
        ),
        out_specs=(P(fsdp, "seq", None), P(fsdp, "seq", None)),
        check_vma=False,
    )
```

```python
import jax
import jax.numpy as jnp
from jax import lax
from jax.experimental import pallas as pl
from jax.experimental.pallas import tpu as pltpu
from jax.sharding import Mesh, PartitionSpec as P

HEADS = 128
HEAD_DIM = 64
GROUPS = 8
STATE = 128
CONV = 4
SPAN = 128
RING = 4
ROWS = 64
WIDTH = 4096
LEN = 256
TENANTS = 4
RANK = 16
FRONT = 512
GROUP_COLS = 1280
BACK = GROUP_COLS - FRONT
GROUP_CHANNELS = 1024
GROUP_HEADS = 16
EXTRA = 128
PANEL = FRONT + EXTRA
NORM_ROWS = 16
DEPTH = 256

eps_norm = 1e-05
eps_column = 1e-06

f32 = jnp.float32
bf16 = jnp.bfloat16


def shift(v, axis, by):
    return lax.ppermute(v, axis, [(i, (i + by) % RING) for i in range(RING)])


def turn(v, axis, by):
    steps = (by, -by)
    return lax.ppermute(
        v,
        ("seq", axis),
        [(k * RING + i, k * RING + (i + steps[k]) % RING) for k in range(2) for i in range(RING)],
    )


def swap(v, axis, near):
    masks = (1, 3) if near else (3, 1)
    return lax.ppermute(
        v,
        ("seq", axis),
        [(k * RING + i, k * RING + (i ^ masks[k])) for k in range(2) for i in range(RING)],
    )


def cross(v):
    return lax.ppermute(v, "seq", [(0, 1), (1, 0)])


def pick(v, index):
    return lax.dynamic_index_in_dim(v, index, 0, keepdims=False)


def place_order(own, right, opposite, left, x):
    twice = jnp.stack([own, right, opposite, left, own, right, opposite, left])
    return lax.dynamic_slice_in_dim(twice, (RING - x) % RING, RING, 0)


def wait_all(ref, sem):
    pltpu.make_async_copy(ref, ref, sem).wait()


def bits(own, at, c):
    gap = own ^ at
    far = gap >> 1
    near = (gap ^ far) & 1
    return jnp.where(c == 0, near, far), jnp.where(c == 0, far, near)


def half_ranges(meta, order, came):
    c, y, z = meta[0], meta[2], meta[3]
    near, far = 1 + 2 * c, 3 - 2 * c
    split = z if order == "yz" else y
    places = [split ^ (came * far) ^ (i * near) for i in range(2)]
    if order == "yz":
        width = RING * DEPTH
        starts = [place * width for place in places]
    else:
        width = DEPTH
        starts = [(at * RING + place) * width for at in range(RING) for place in places]
    return [pl.multiple_of(start, DEPTH) for start in starts], width


def half_copies(meta, order, panel_refs, panel, sem):
    other = meta[2] if order == "yz" else meta[3]
    for at in range(RING):
        first, second = bits(other, at, meta[0])
        for i in range(2):
            slot = i * RING + at if order == "yz" else at * 2 + i
            for half in range(2):

                @pl.when(second == half)
                def _(i=i, half=half, first=first, slot=slot):
                    pltpu.make_async_copy(
                        panel_refs[half].at[first + 2 * i, pl.ds(0, DEPTH), :], panel.at[slot], sem
                    ).start()


def piece_copies(tok_refs, pieces, sem):
    for i, ref in enumerate(tok_refs):
        pltpu.make_async_copy(ref, pieces.at[i], sem.at[i]).start()


def half_products(meta, order, came, pieces, piece_sem, panel, emit):
    c = meta[0]
    starts, width = half_ranges(meta, order, came)
    for source, place in ((0, c), (1, 1 - c)):
        sequences = (0, 1 + place, 2 - place, 3)
        for i, sequence in enumerate(sequences):
            at = 4 * source + i
            if piece_sem is not None:
                wait_all(pieces.at[at], piece_sem.at[at])
            rows = pl.ds(pl.multiple_of(sequence * LEN + place * SPAN, SPAN), SPAN)
            piece = jnp.concatenate([pieces[at, :, pl.ds(start, width)] for start in starts], axis=1)
            whole = panel[...].reshape(WIDTH // 2, panel.shape[-1])
            emit(rows, jnp.dot(piece, whole, preferred_element_type=f32))


def project_held(meta, *refs):
    tok_refs, front_ref, back_ref = refs[:8], refs[8:10], refs[10:12]
    front_out, back_out, front_panel, back_panel, pieces, sem, piece_sem = refs[12:]
    parts = (("yz", front_ref, front_panel, front_out), ("zy", back_ref, back_panel, back_out))
    for i, (order, ref, panel, _) in enumerate(parts):
        half_copies(meta, order, ref, panel, sem.at[i])
        if i == 0:
            piece_copies(tok_refs, pieces, piece_sem)
    for i, (order, _, panel, out) in enumerate(parts):
        wait_all(panel, sem.at[i])

        def emit(rows, product, out=out):
            out[rows, :] = product

        half_products(meta, order, 0, pieces, piece_sem if i == 0 else None, panel, emit)


def project_came(meta, *refs):
    tok_refs, front_held, front_ref, back_ref = refs[:8], refs[8:10], refs[10:12], refs[12:14]
    up_ref, mag_ref, bias_ref, rate_ref, front_base, back_base = refs[14:20]
    outs = refs[20:24]
    step_out, cumul_out, cumul_t_out = refs[24:27]
    front_panel, back_panel, pieces, front_acc, back_acc, ready, norms = refs[27:34]
    sem, piece_sem, ready_sem, norm_sem = refs[34:]
    c = meta[0]
    for i, ref in enumerate((*front_held, *front_ref)):
        pltpu.make_async_copy(
            ref.at[:, pl.ds(DEPTH, NORM_ROWS), :], norms.at[pl.ds(4 * i, 4)], norm_sem
        ).start()
    parts = (
        ("yz", front_ref, front_panel, front_base, front_acc),
        ("zy", back_ref, back_panel, back_base, back_acc),
    )
    for i, (order, ref, panel, _, _) in enumerate(parts):
        half_copies(meta, order, ref, panel, sem.at[i])
        if i == 0:
            piece_copies(tok_refs, pieces, piece_sem)
    wait_all(norms, norm_sem)
    total = jnp.sum(norms[...].astype(f32), axis=0)
    squares = [total[8 * i : 8 * i + 4] + total[8 * i + 4 : 8 * i + 8] for i in range(2)]
    squares = jnp.concatenate(squares, axis=1)
    scale = mag_ref[...] / jnp.sqrt(squares + eps_column)
    up = padded_up(up_ref)
    for i, (order, _, panel, base, acc) in enumerate(parts):
        wait_all(panel, sem.at[i])

        def emit(rows, product, base=base, acc=acc):
            acc[rows, :] = base[rows, :] + product

        half_products(meta, order, 1, pieces, piece_sem if i == 0 else None, panel, emit)
    lane_tenant = lax.broadcasted_iota(jnp.int32, (LEN, EXTRA), 1) // RANK - RING
    for s in (1, 2, 3, 0):
        tenant = meta[4 + s]
        rows = pl.ds(s * LEN, LEN)
        low = jnp.where(lane_tenant == tenant, front_acc[rows, FRONT:], 0.0).astype(bf16)
        for acc, cols in ((front_acc, slice(0, FRONT)), (back_acc, slice(FRONT, GROUP_COLS))):
            result = acc[rows, : cols.stop - cols.start] + jnp.dot(
                low, up[:, cols], preferred_element_type=f32
            )
            ready[s, :, cols] = (result * tenant_row(scale[:, cols], tenant)).astype(bf16)
        pltpu.make_async_copy(ready.at[s], outs[s], ready_sem.at[s]).start()
    heads_here = HEADS // 2
    bias = jnp.where(c == 0, bias_ref[:, :heads_here], bias_ref[:, heads_here:])
    rate = jnp.where(c == 0, rate_ref[:, :heads_here], rate_ref[:, heads_here:])
    raw = front_acc[0:LEN, FRONT : FRONT + heads_here] + bias
    step = jnp.maximum(raw, 0.0) + jnp.log1p(jnp.exp(-jnp.abs(raw)))
    logdecay = -step * jnp.exp(rate)
    ones = jnp.where(
        lax.broadcasted_iota(jnp.int32, (SPAN, SPAN), 0)
        >= lax.broadcasted_iota(jnp.int32, (SPAN, SPAN), 1),
        1.0,
        0.0,
    )
    for block in range(LEN // SPAN):
        rows = slice(block * SPAN, (block + 1) * SPAN)
        cumul = jnp.dot(
            ones, logdecay[rows], precision=lax.Precision.HIGHEST, preferred_element_type=f32
        )
        cumul_t = cumul.T
        for g in range(RING):
            heads = slice(g * GROUP_HEADS, (g + 1) * GROUP_HEADS)
            step_out[g, rows, :] = step[rows, heads]
            cumul_out[g, rows, :] = cumul[:, heads]
            cumul_t_out[g, :, rows] = cumul_t[heads, :]
    for s in range(RING):
        pltpu.make_async_copy(ready.at[s], outs[s], ready_sem.at[s]).wait()


def padded_up(up_ref):
    return jnp.concatenate([jnp.zeros((EXTRA - TENANTS * RANK, GROUP_COLS), bf16), up_ref[...]], axis=0)


def tenant_row(table, tenant):
    row = table[0:1]
    for k in range(1, TENANTS):
        row = jnp.where(tenant == k, table[k : k + 1], row)
    return row


def hbm_specs(n):
    return [pl.BlockSpec(memory_space=pltpu.HBM)] * n


def vmem_specs(n):
    return [pl.BlockSpec(memory_space=pltpu.VMEM)] * n


def half_scratch():
    return [
        pltpu.VMEM((8, DEPTH, PANEL), bf16),
        pltpu.VMEM((8, DEPTH, BACK), bf16),
        pltpu.VMEM((8, SPAN, WIDTH), bf16),
    ]


def run_held(meta, tok, front, back):
    rows = RING * LEN
    return pl.pallas_call(
        project_held,
        in_specs=[pl.BlockSpec(memory_space=pltpu.SMEM)] + hbm_specs(12),
        out_specs=vmem_specs(2),
        out_shape=[jax.ShapeDtypeStruct((rows, n), f32) for n in (PANEL, BACK)],
        scratch_shapes=half_scratch()
        + [pltpu.SemaphoreType.DMA((2,)), pltpu.SemaphoreType.DMA((8,))],
        compiler_params=pltpu.CompilerParams(vmem_limit_bytes=48 << 20),
        cost_estimate=pl.CostEstimate(
            flops=rows * WIDTH * (PANEL + BACK), bytes_accessed=20 << 20, transcendentals=0
        ),
        name="project_held",
    )(meta, *tok, *front, *back)


def run_came(meta, tok, front, front_came, back_came, up, mag, bias, rate, bases):
    rows = RING * LEN
    heads = jax.ShapeDtypeStruct((RING, LEN, GROUP_HEADS), f32)
    return pl.pallas_call(
        project_came,
        grid_spec=pltpu.PrefetchScalarGridSpec(
            num_scalar_prefetch=1,
            grid=(1,),
            in_specs=hbm_specs(14)
            + [
                pl.BlockSpec((TENANTS * RANK, GROUP_COLS), lambda i, m: (0, m[1])),
                pl.BlockSpec((TENANTS, GROUP_COLS), lambda i, m: (0, m[1])),
            ]
            + vmem_specs(4),
            out_specs=hbm_specs(4) + vmem_specs(3),
            scratch_shapes=half_scratch()
            + [
                pltpu.VMEM((rows, PANEL), f32),
                pltpu.VMEM((rows, BACK), f32),
                pltpu.VMEM((RING, LEN, GROUP_COLS), bf16),
                pltpu.VMEM((16, NORM_ROWS, PANEL), bf16),
                pltpu.SemaphoreType.DMA((2,)),
                pltpu.SemaphoreType.DMA((8,)),
                pltpu.SemaphoreType.DMA((RING,)),
                pltpu.SemaphoreType.DMA,
            ],
        ),
        out_shape=[jax.ShapeDtypeStruct((LEN, GROUP_COLS), bf16)] * RING
        + [heads, heads, jax.ShapeDtypeStruct((RING, GROUP_HEADS, LEN), f32)],
        compiler_params=pltpu.CompilerParams(vmem_limit_bytes=48 << 20),
        cost_estimate=pl.CostEstimate(
            flops=rows * WIDTH * (PANEL + BACK), bytes_accessed=20 << 20, transcendentals=0
        ),
        name="project_came",
    )(meta, *tok, *front, *front_came, *back_came, up, mag, bias, rate, *bases)


def contract_first(a, b):
    return lax.dot_general(a, b, (((0,), (0,)), ((), ())), preferred_element_type=f32)


def contract_last(a, b):
    return lax.dot_general(a, b, (((1,), (1,)), ((), ())), preferred_element_type=f32)


def scan_kernel(aliased, meta, *refs):
    projected, taps, offset, gain, skip, step_ref, cumul_ref, cumul_t_ref, cot_own, cot_other = refs[:10]
    refs = refs[10 + aliased :]
    mixed_ref, grad_ref, send_ref = refs[:3]
    padded, conv, raws, grads, incoming, outgoing, mixed_all, x_all, steps, boths, mixes = refs[3:]
    c, length = meta[0], meta[2]
    pairs = GROUP_HEADS // 2
    padded[0:8, :] = jnp.zeros((8, GROUP_COLS), f32)
    padded[8:, :] = projected[...].astype(f32)
    summed = offset[...] + taps[0:1, :] * padded[5 : 5 + LEN, :]
    for i in range(1, CONV):
        summed = summed + taps[i : i + 1, :] * padded[5 + i : 5 + i + LEN, :]
    conv[...] = (summed / (1.0 + jnp.exp(-summed))).astype(bf16)
    causal = lax.broadcasted_iota(jnp.int32, (SPAN, SPAN), 0) >= lax.broadcasted_iota(
        jnp.int32, (SPAN, SPAN), 1
    )
    anti = lax.broadcasted_iota(jnp.int32, (SPAN, SPAN), 0) <= lax.broadcasted_iota(
        jnp.int32, (SPAN, SPAN), 1
    )
    low_lane = lax.broadcasted_iota(jnp.int32, (SPAN, SPAN), 1) < HEAD_DIM

    def spread(ref, rows, head):
        return jnp.broadcast_to(ref[0, rows, head : head + 1], (SPAN, SPAN))

    def stacked(values):
        zero = jnp.zeros_like(values)
        return jnp.concatenate(
            [jnp.where(low_lane, values, zero), jnp.where(low_lane, zero, values)], axis=0
        )

    for block in range(LEN // SPAN):
        rows = slice(block * SPAN, (block + 1) * SPAN)
        keys = conv[rows, GROUP_CHANNELS : GROUP_CHANNELS + STATE]
        queries = conv[rows, GROUP_CHANNELS + STATE :]
        scores = jnp.where(causal, contract_last(queries, keys), 0.0)
        squares = jnp.zeros((SPAN, SPAN), f32)
        for q in range(pairs):
            lanes = slice(q * SPAN, (q + 1) * SPAN)
            values = conv[rows, lanes].astype(f32)
            level = [spread(cumul_ref, rows, 2 * q + i) for i in range(2)]
            mix = [
                (
                    jnp.exp(jnp.minimum(level[i] - cumul_t_ref[0, 2 * q + i : 2 * q + i + 1, rows], 0.0))
                    * scores
                ).astype(bf16)
                for i in range(2)
            ]
            step = jnp.where(low_lane, spread(step_ref, rows, 2 * q), spread(step_ref, rows, 2 * q + 1))
            steps[rows, lanes] = step
            inflow = (step * values).astype(bf16)
            mixes[block, q, :SPAN] = mix[0]
            mixes[block, q, SPAN:] = mix[1]
            raw = jnp.dot(
                jnp.concatenate(mix, axis=1), stacked(inflow), preferred_element_type=f32
            )
            both = jnp.where(low_lane, level[0], level[1])
            if block == 0:
                tail = jnp.exp(both[SPAN - 1 :, :] - both)
                boths[rows, lanes] = tail
                scaled = (inflow.astype(f32) * tail).astype(bf16)
                incoming[:, lanes] = contract_first(keys, scaled).astype(bf16)
            else:
                growth = jnp.exp(both)
                boths[rows, lanes] = growth
                raw = raw + jnp.dot(
                    queries, incoming[:, lanes], preferred_element_type=f32
                ) * growth
            raw = raw + skip[:, lanes] * values
            raws[rows, lanes] = raw
            squares = squares + raw * raw
        mean_sq = jnp.sum(squares, axis=1, keepdims=True) / GROUP_CHANNELS
        inverse = lax.rsqrt(mean_sq + eps_norm)
        at = block * SPAN + lax.broadcasted_iota(jnp.int32, (SPAN, 1), 0)
        live = jnp.where(at < length, 1.0, 0.0)
        upstream = jnp.where(c == block, cot_own[...], cot_other[...]).astype(f32) * live
        raw = raws[rows, :]
        scaled_up = upstream * gain[...]
        mixed_all[rows, :] = ((gain[...] * raw) * (inverse * live)).astype(bf16)
        along = jnp.sum(scaled_up * raw, axis=1, keepdims=True) / GROUP_CHANNELS
        grads[rows, :] = scaled_up * inverse - raw * (along * inverse * inverse * inverse)

    for block in reversed(range(LEN // SPAN)):
        rows = slice(block * SPAN, (block + 1) * SPAN)
        keys = conv[rows, GROUP_CHANNELS : GROUP_CHANNELS + STATE]
        queries = conv[rows, GROUP_CHANNELS + STATE :]
        for q in range(pairs):
            lanes = slice(q * SPAN, (q + 1) * SPAN)
            step = steps[rows, lanes]
            grad = grads[rows, lanes]
            back = contract_first(mixes[block, q], stacked(grad.astype(bf16)))
            if block == 1:
                weighted = (grad * boths[rows, lanes]).astype(bf16)
                outgoing[:, lanes] = contract_first(queries, weighted).astype(bf16)
            else:
                back = back + jnp.dot(
                    keys, outgoing[:, lanes], preferred_element_type=f32
                ) * boths[rows, lanes]
            x_all[rows, lanes] = (skip[:, lanes] * grad + step * back).astype(bf16)

    mine = pl.ds(pl.multiple_of(c * SPAN, SPAN), SPAN)
    others = pl.ds(pl.multiple_of((1 - c) * SPAN, SPAN), SPAN)
    mixed_ref[...] = mixed_all[mine, :]
    grad_ref[...] = x_all[mine, :]
    send_ref[0] = mixed_all[others, :]
    send_ref[1] = x_all[others, :]


def run_scan(d, meta, projected, shared, cot, cot_other, totals):
    taps, offset, gain, skip, step, cumul, cumul_t = shared
    out_full = jax.ShapeDtypeStruct((SPAN, GROUPS * GROUP_CHANNELS), bf16)

    def local(m):
        return (m[1] + d) % RING

    def whole(m):
        return m[0] * RING + local(m)

    aliased = 0 if totals is None else 2
    extra = () if totals is None else tuple(totals)

    def kernel(*refs):
        scan_kernel(aliased, *refs)

    return pl.pallas_call(
        kernel,
        grid_spec=pltpu.PrefetchScalarGridSpec(
            num_scalar_prefetch=1,
            grid=(1,),
            in_specs=[
                pl.BlockSpec((LEN, GROUP_COLS), lambda i, m: (0, 0)),
                pl.BlockSpec((CONV, GROUP_COLS), lambda i, m: (0, whole(m))),
                pl.BlockSpec((1, GROUP_COLS), lambda i, m: (0, whole(m))),
                pl.BlockSpec((1, GROUP_CHANNELS), lambda i, m: (0, whole(m))),
                pl.BlockSpec((1, GROUP_CHANNELS), lambda i, m: (0, whole(m))),
                pl.BlockSpec((1, LEN, GROUP_HEADS), lambda i, m: (local(m), 0, 0)),
                pl.BlockSpec((1, LEN, GROUP_HEADS), lambda i, m: (local(m), 0, 0)),
                pl.BlockSpec((1, GROUP_HEADS, LEN), lambda i, m: (local(m), 0, 0)),
                pl.BlockSpec((SPAN, GROUP_CHANNELS), lambda i, m: (0, whole(m))),
                pl.BlockSpec((SPAN, GROUP_CHANNELS), lambda i, m: (0, local(m))),
            ]
            + hbm_specs(aliased),
            out_specs=[
                pl.BlockSpec((SPAN, GROUP_CHANNELS), lambda i, m: (0, whole(m))),
                pl.BlockSpec((SPAN, GROUP_CHANNELS), lambda i, m: (0, whole(m))),
                pl.BlockSpec((2, SPAN, GROUP_CHANNELS), lambda i, m: (0, 0, 0)),
            ],
            scratch_shapes=[
                pltpu.VMEM((LEN + 8, GROUP_COLS), f32),
                pltpu.VMEM((LEN, GROUP_COLS), bf16),
                pltpu.VMEM((LEN, GROUP_CHANNELS), f32),
                pltpu.VMEM((LEN, GROUP_CHANNELS), f32),
                pltpu.VMEM((STATE, GROUP_CHANNELS), bf16),
                pltpu.VMEM((STATE, GROUP_CHANNELS), bf16),
                pltpu.VMEM((LEN, GROUP_CHANNELS), bf16),
                pltpu.VMEM((LEN, GROUP_CHANNELS), bf16),
                pltpu.VMEM((LEN, GROUP_CHANNELS), f32),
                pltpu.VMEM((LEN, GROUP_CHANNELS), f32),
                pltpu.VMEM((2, GROUP_HEADS // 2, 2 * SPAN, SPAN), bf16),
            ],
        ),
        out_shape=[out_full, out_full, jax.ShapeDtypeStruct((2, SPAN, GROUP_CHANNELS), bf16)],
        input_output_aliases={} if totals is None else {11: 0, 12: 1},
        compiler_params=pltpu.CompilerParams(vmem_limit_bytes=60 << 20),
        cost_estimate=pl.CostEstimate(flops=6 << 30, bytes_accessed=4 << 20, transcendentals=0),
        name="scan_group",
    )(meta, projected, taps, offset, gain, skip, step, cumul, cumul_t, cot, cot_other, *extra)


def split_sum(values):
    high = lax.reduce_precision(values, 8, 7)
    return high.astype(bf16), (values - high).astype(bf16)


def norm_rows(sums):
    high, low = split_sum(sums)
    parts = [part[..., i * PANEL : (i + 1) * PANEL] for i in range(2) for part in (high, low)]
    return jnp.concatenate(parts, axis=-2)


def per_device(
    tokens,
    weight,
    adapter_down_weight,
    adapter_up_weight,
    magnitude,
    step_size_weight,
    step_size_bias,
    decay_rate_log,
    head_skip_gain,
    convolution_weight,
    convolution_bias,
    grouped_norm_gain,
    tenant,
    lengths,
    cotangent,
):
    c, x, y, z = (lax.axis_index(name) for name in ("seq", "x", "y", "z"))
    own_tokens = tokens[0]
    upstream = cotangent[0]
    by_chip = jnp.swapaxes(weight.reshape(ROWS, RING, GROUP_COLS), 0, 1)

    def round_x(block):
        return [
            block[0],
            shift(block[3], "x", -1),
            shift(block[2], "x", 2),
            shift(block[1], "x", 1),
        ]

    tie = lax.optimization_barrier

    def grown(part, axis, near):
        return jnp.concatenate([part, swap(part, axis, near)], axis=0)

    adapted = weight.astype(f32)[None] + jnp.einsum(
        "gbc,bco->bgo", adapter_down_weight, adapter_up_weight, preferred_element_type=f32
    )
    sums = jnp.sum(adapted * adapted, axis=1).reshape(TENANTS, RING, GROUP_COLS)
    marks = norm_rows(jnp.swapaxes(sums, 0, 1))
    heads_here = HEADS // 2
    extras = jnp.concatenate(
        [
            lax.dynamic_slice_in_dim(step_size_weight, c * heads_here, heads_here, 1),
            adapter_down_weight.reshape(ROWS, TENANTS * RANK),
        ],
        axis=1,
    )
    tenant_mark = jnp.broadcast_to(tenant[0].astype(bf16), (RING, NORM_ROWS, EXTRA))
    back_mark = jnp.zeros((RING, NORM_ROWS, BACK), bf16)
    blocks = jnp.concatenate(
        [
            jnp.concatenate(
                [
                    by_chip[:, :, :FRONT],
                    jnp.broadcast_to(extras, (RING, ROWS, EXTRA)),
                    by_chip[:, :, FRONT:],
                ],
                axis=2,
            ),
            jnp.concatenate([marks, tenant_mark, back_mark[:, :, EXTRA:]], axis=2),
        ],
        axis=1,
    )

    blocks = round_x([pick(blocks, (x + d) % RING) for d in range(RING)])
    tenants = [tenant[0]] + [blocks[i][ROWS, PANEL].astype(jnp.int32) for i in (3, 1, 2)]
    rows = place_order(*[part[:ROWS] for part in blocks], x).reshape(DEPTH, GROUP_COLS + EXTRA)
    sums = sum(part[ROWS:, :PANEL].astype(f32) for part in blocks)
    sums = jnp.concatenate([sums[0:4] + sums[4:8], sums[8:12] + sums[12:16]], axis=1)
    front = jnp.concatenate([rows[:, :PANEL], norm_rows(sums)], axis=0)[None]
    back = rows[None, :, PANEL:]

    def grown(part, axis, near):
        return jnp.concatenate([part, swap(part, axis, near)], axis=0)

    per_core = GROUPS // 2 * GROUP_CHANNELS
    cot_other = lax.dynamic_slice_in_dim(upstream, (1 - c) * per_core, per_core, 1)
    front, back, own_tokens, cot_other = tie((front, back, own_tokens, cot_other))
    crossed, cot_other = [cross(own_tokens)], cross(cot_other)
    front, back = grown(front, "y", True), grown(back, "z", True)
    front, back, own_tokens, crossed, cot_other = tie((front, back, own_tokens, crossed, cot_other))
    one = turn(own_tokens, "x", 1)
    front, back = grown(front, "z", True), grown(back, "y", True)
    front, back, one, own_tokens = tie((front, back, one, own_tokens))
    two = turn(own_tokens, "x", -1)
    crossed = crossed + [cross(one)]
    front, back = [front, swap(front, "y", False)], [back, swap(back, "z", False)]
    front, back, one, two, crossed = tie((front, back, one, two, crossed))
    three = turn(one, "x", 1)
    front_came = [swap(part, "z", False) for part in front]
    back_came = [swap(part, "y", False) for part in back]
    crossed = crossed + [cross(two), cross(three)]

    up = adapter_up_weight.reshape(TENANTS * RANK, RING * GROUP_COLS)
    place = jnp.stack([c, x, y, z]).astype(jnp.int32)
    meta = jnp.concatenate([place, jnp.stack(tenants)])
    tok = [own_tokens, one, two, three] + crossed
    bases = run_held(place, tok, front, back)
    *projected, step_size, cumul, cumul_t = run_came(
        meta,
        tok,
        front,
        front_came,
        back_came,
        up,
        magnitude,
        step_size_bias[None],
        decay_rate_log[None],
        bases,
    )
    shared = (
        convolution_weight,
        convolution_bias[None],
        grouped_norm_gain[None],
        jnp.repeat(head_skip_gain, HEAD_DIM)[None],
        step_size,
        cumul,
        cumul_t,
    )

    own, to_left, to_right, to_opposite = projected
    from_right, from_left = shift(to_left, "x", -1), shift(to_right, "x", 1)
    to_opposite = tie((to_opposite, from_left, from_right))[0]
    projected = [own, from_right, from_left, shift(to_opposite, "x", 2)]
    def written(totals, group, got):
        at = (RING * (1 - c) + group) * GROUP_CHANNELS
        return [lax.dynamic_update_slice_in_dim(v, part, at, 1) for v, part in zip(totals, got)]

    totals = None
    waiting = []
    scan_meta = jnp.stack([c, x, lengths[0]]).astype(jnp.int32)
    for i, d in ((0, 0), (1, 1), (2, 3), (3, 2)):
        if i == 3:
            for group, got in waiting[:2]:
                totals = written(totals, group, got)
            waiting = waiting[2:]
        *totals, send = run_scan(d, scan_meta, projected[i], shared, upstream, cot_other, totals)
        waiting.append(((x + d) % RING, cross(send)))
    for group, got in waiting:
        totals = written(totals, group, got)
    mixed, x_grad = totals
    return (mixed[None], x_grad[None])


def solution(mesh):
    chips = Mesh(mesh.devices.reshape(2, RING, RING, RING), ("seq", "z", "y", "x"))
    fsdp = ("z", "y", "x")
    return jax.shard_map(
        per_device,
        mesh=chips,
        in_specs=(
            P(fsdp, "seq", None),
            P(fsdp, "seq"),
            P(fsdp, None, None),
            P(None, None, "seq"),
            P(None, "seq"),
            P(fsdp, None),
            P(),
            P(),
            P(),
            P(),
            P(),
            P(),
            P(fsdp),
            P(fsdp),
            P(fsdp, "seq", None),
        ),
        out_specs=(P(fsdp, "seq", None), P(fsdp, "seq", None)),
        check_vma=False,
    )
```
